128 devices in a mesh: patch: 64 (over z, y, x), batch: 2 (over core).
Axes of the slice: x: 4, y: 4, z: 4, core: 2. Of those that a mesh axis runs over, the one named last changes fastest.
Arguments:
- tokens: bfloat16 [16384, 1152], P(('batch', 'patch')), parts along dimension 0, may hold values from -6 to 6
- slots: int32 [16384], P(('batch', 'patch')), parts along dimension 0, may hold values from 0 to 127, as said below
- counts: int32 [128], P(('batch', 'patch')), parts along dimension 0, may hold values from 32 to 128, as said below
- shift: float32 [1152], replicated, may hold values from -3 to 3
- scale: float32 [1152], replicated, may hold values from -3 to 3
- gate: float32 [1152], replicated, may hold values from -4 to 4
- w_qkv: bfloat16 [1152, 3456], replicated, may hold values from -1 to 1
- w_out: bfloat16 [1152, 1152], replicated, may hold values from -0.1875 to 0.1875
Outputs:
- result: bfloat16 [16384, 1152], P(('batch', 'patch')), parts along dimension 0
The draws below stay inside these ranges and needn't reach their ends.
There are 2 independent parts, one for each index of `batch`. The reference program is written for one: setup_inputs(seed, part) draws one part's arguments, and reference() takes and returns one part's arrays. A program takes and returns all parts, laid end to end along the dimension named above; an argument that names none is the same for every part. Nothing has to cross between parts.
Inputs may be any that keep to these rules, and one draw needn't show every extreme that they name: `counts`: at least a quarter of each block's slots are live. The live slots of all blocks of an image number exactly 80 times the number of patch devices, and all blocks of some device are full. `slots`: every token's slot is below its block's count, and every slot below the count holds at least one token.
All inputs are finite; a program needn't handle non-finite values.
Results may differ from the reference program's by a relative error of at most 0.011.
Values may be sent and summed in bfloat16 or wider, within the bound.
No kernel may reach another device: no remote copies, remote signals or barrier semaphores. Data moves between devices by JAX's collectives and lax.ppermute only.
A program may use at most 192 MiB of HBM per device.

```python
import jax
import jax.numpy as jnp
from jax import lax

D = 1152
HEADS = 16
HD = 72
BLK = 128
BLK_DEV = 1
TOKENS = 8192


def merge_plan(key):
    block_total = TOKENS // BLK
    device_total = block_total // BLK_DEV
    extra = BLK - BLK // 4
    needed = 5 * TOKENS // 8 - block_total * (BLK // 4)
    base = jax.random.fold_in(key, 11)
    key_level, key_full, key_noise, key_perm, key_rest = jax.random.split(base, 5)
    level = jax.random.randint(key_level, (block_total,), 0, 4096).astype(jnp.int32)
    chosen = jax.random.randint(key_full, (), 0, device_total).astype(jnp.int32)
    owner = jnp.arange(block_total, dtype=jnp.int32) // BLK_DEV
    level = jnp.where(owner == chosen, 8192, level).astype(jnp.int32)
    noise = jax.random.randint(key_noise, (block_total, extra), 0, 4096).astype(jnp.int32)
    ranked = ((level[:, None] + noise) * (block_total * extra)).reshape(block_total * extra) + jnp.arange(block_total * extra, dtype=jnp.int32)
    ordered = jnp.sort(ranked)
    cutoff = ordered[block_total * extra - needed]
    picked = (ranked >= cutoff).astype(jnp.int32).reshape(block_total, extra)
    counts = (BLK // 4 + jnp.sum(picked, axis=1)).astype(jnp.int32)
    ranks = jax.vmap(lambda k: jax.random.permutation(k, BLK))(jax.random.split(key_perm, block_total)).astype(jnp.int32)
    spare = jax.random.randint(key_rest, (block_total, BLK), 0, BLK * BLK).astype(jnp.int32) % counts[:, None]
    slots = jnp.where(ranks < counts[:, None], ranks, spare).astype(jnp.int32)
    return (slots.reshape(TOKENS), counts)


def draw_slots(key, part):
    return merge_plan(key)[0]


def draw_counts(key, part):
    return merge_plan(key)[1]


def draw_tokens(key, part):
    key_base = jax.random.fold_in(jax.random.fold_in(key, 23), 0)
    drawn = jnp.clip(jax.random.normal(key_base, (TOKENS, D), jnp.float32), -6.0, 6.0)
    return drawn.astype(jnp.bfloat16)


def draw_w_qkv(key, part):
    key_base = jax.random.fold_in(jax.random.fold_in(key, 37), 0)
    base = jnp.clip(jax.random.normal(key_base, (D, 3 * D), jnp.float32), -6.0, 6.0) * D ** (-0.5)
    return jnp.clip(base, -1.0, 1.0).astype(jnp.bfloat16)


def gaussian(own_key, extent, deviation, limit, kind=jnp.bfloat16):
    drawn = jax.random.normal(own_key, extent, jnp.float32) * deviation
    return jnp.minimum(jnp.maximum(drawn, -limit), limit).astype(kind)


def setup_inputs(seed: int = 0, part: int = 0) -> dict:
    key_of = jax.random.split(jax.random.key(seed), 9)
    part_splits = jax.random.split(jax.random.fold_in(key_of[8], part), 9)
    tokens = draw_tokens(jax.random.fold_in(jax.random.fold_in(key_of[8], part), 71), part)
    slots = draw_slots(jax.random.fold_in(jax.random.fold_in(key_of[8], part), 71), part)
    counts = draw_counts(jax.random.fold_in(jax.random.fold_in(key_of[8], part), 71), part)
    shift = gaussian(key_of[3], (D,), 0.5, 3.0, jnp.float32)
    scale = gaussian(key_of[4], (D,), 0.5, 3.0, jnp.float32)
    gate = gaussian(key_of[5], (D,), 1.0, 4.0, jnp.float32)
    w_qkv = draw_w_qkv(jax.random.fold_in(key_of[8], 71), part)
    w_out = gaussian(key_of[7], (D, D), D ** -0.5, 0.1875)
    return dict(tokens=tokens, slots=slots, counts=counts, shift=shift, scale=scale, gate=gate, w_qkv=w_qkv, w_out=w_out)


def layer_norm(merged, shift, scale):
    values = merged.astype(jnp.float32)
    center = lax.optimization_barrier(jnp.mean(values, axis=-1, keepdims=True))
    spread = lax.optimization_barrier(jnp.mean((values - center) ** 2, axis=-1, keepdims=True))
    return ((values - center) * lax.rsqrt(spread + 1e-06) * (1.0 + scale) + shift).astype(jnp.bfloat16)

def reference(tokens, slots, counts, shift, scale, gate, w_qkv, w_out):
    nblk = TOKENS // BLK
    onehot = (slots.reshape(nblk, BLK)[:, :, None] == jnp.arange(BLK, dtype=jnp.int32)[None, None, :]).astype(jnp.float32)
    sums = jnp.einsum('bts,btd->bsd', onehot, tokens.reshape(nblk, BLK, D).astype(jnp.float32))
    members = lax.optimization_barrier(jnp.sum(onehot, axis=1))
    merged = (sums / jnp.maximum(members, 1.0)[:, :, None]).astype(jnp.bfloat16).reshape(TOKENS, D)
    normed = layer_norm(merged, shift, scale)
    qkv = jnp.dot(normed, w_qkv, preferred_element_type=jnp.float32)
    query = qkv[:, :D].astype(jnp.bfloat16).reshape(TOKENS, HEADS, HD).transpose(1, 0, 2)
    keys = qkv[:, D:2 * D].astype(jnp.bfloat16).reshape(TOKENS, HEADS, HD).transpose(1, 0, 2)
    values = qkv[:, 2 * D:].astype(jnp.bfloat16).reshape(TOKENS, HEADS, HD).transpose(1, 0, 2)
    live = (jnp.arange(BLK, dtype=jnp.int32)[None, :] < counts[:, None]).reshape(TOKENS)
    bias = jnp.where(live, jnp.log(jnp.maximum(members.reshape(TOKENS), 1.0)), -1e+30).astype(jnp.float32)
    inverse = 1.0 / HD ** 0.5

    def one_head(items):
        qh, kh, vh = items
        score = jnp.dot(qh, kh.T, preferred_element_type=jnp.float32) * inverse + bias[None, :]
        top = lax.optimization_barrier(jnp.max(score, axis=-1, keepdims=True))
        probs = jnp.exp(score - top)
        total = lax.optimization_barrier(jnp.sum(probs, axis=-1, keepdims=True))
        return jnp.dot(probs.astype(jnp.bfloat16), vh, preferred_element_type=jnp.float32) / total
    heads_out = lax.map(one_head, (query, keys, values))
    attended = heads_out.transpose(1, 0, 2).reshape(TOKENS, D).astype(jnp.bfloat16)
    projected = jnp.dot(attended, w_out, preferred_element_type=jnp.float32)
    branch = jnp.einsum('bts,bsd->btd', onehot, projected.reshape(nblk, BLK, D), precision=lax.Precision.HIGHEST).reshape(TOKENS, D)
    return (tokens.astype(jnp.float32) + gate * branch).astype(jnp.bfloat16)
```

```python
import jax
import jax.numpy as jnp
from jax import lax
from jax.experimental import pallas as pl
from jax.experimental.pallas import tpu as pltpu
from jax.sharding import PartitionSpec as P

D = 1152
HEADS = 16
HD = 72
BLK = 128
HALF = BLK // 2
DEVICES = 64
GROUPS = DEVICES // HEADS

IN_ROWS = 112
OUT_ROWS = 40
AUG = 80
TILES = 22
WIDE = 2 * BLK
COLUMNS = TILES * BLK
W_CHUNK = 384
W_CHUNKS = 3 * D // W_CHUNK
VMEM = 56 * 1024 * 1024

INVERSE = 1.0 / HD**0.5
LOG2E = 1.4426950408889634


def place_of(slots):
    return (slots & 1) * HALF + (slots >> 1)


def roll(x, shift):
    return pltpu.roll(x, shift, 1)


def pre_kernel(
    counts_ref, slots_ref, tokens_ref, shift_ref, scale_ref, w_ref, out_ref, w_buf, qkv_t, sems
):
    copies = [
        pltpu.make_async_copy(
            w_ref.at[:, pl.ds(c * W_CHUNK, W_CHUNK)], w_buf.at[c], sems.at[c]
        )
        for c in range(W_CHUNKS)
    ]
    for copy in copies:
        copy.start()
    place = jnp.broadcast_to(place_of(slots_ref[...]), (BLK, BLK))
    row_id = lax.broadcasted_iota(jnp.int32, (BLK, BLK), 0)
    hot = jnp.where(place == row_id, 1.0, 0.0)
    members = jnp.sum(hot, axis=1, keepdims=True)
    sums = jnp.dot(hot.astype(jnp.bfloat16), tokens_ref[...], preferred_element_type=jnp.float32)
    values = (sums / jnp.maximum(members, 1.0)).astype(jnp.bfloat16).astype(jnp.float32)
    center = jnp.mean(values, axis=-1, keepdims=True)
    off = values - center
    spread = jnp.mean(off * off, axis=-1, keepdims=True)
    normed = (off * lax.rsqrt(spread + 1e-06) * (1.0 + scale_ref[...]) + shift_ref[...]).astype(
        jnp.bfloat16
    )
    for c in range(W_CHUNKS):
        copies[c].wait()
        part = jnp.dot(normed, w_buf[c], preferred_element_type=jnp.float32)
        for t in range(W_CHUNK // BLK):
            at = c * W_CHUNK + t * BLK
            qkv_t[at : at + BLK, :] = part[:, t * BLK : (t + 1) * BLK].T

    members_row = jnp.sum(hot.T, axis=0, keepdims=True)
    low = lax.broadcasted_iota(jnp.int32, (1, BLK), 1) < HALF
    line = lax.broadcasted_iota(jnp.int32, (8, BLK), 0)
    count = counts_ref[0]
    live = [((count + 1) >> 1).astype(jnp.float32), (count >> 1).astype(jnp.float32)]
    sizes_of = [roll(jnp.broadcast_to(members_row, (8, BLK)), HALF)]
    sizes_of.append(jnp.broadcast_to(members_row, (8, BLK)))
    sizes = [
        [
            jnp.where(
                line == 0,
                sizes_of[b],
                jnp.where(line == 1, live[b], jnp.where(line == 2, live[a], 0.0)),
            )
            for b in range(2)
        ]
        for a in range(2)
    ]
    for h in range(HEADS):
        q = qkv_t[h * HD : (h + 1) * HD, :]
        k = qkv_t[D + h * HD : D + (h + 1) * HD, :]
        v = qkv_t[2 * D + h * HD : 2 * D + (h + 1) * HD, :]
        q_roll, k_roll, v_roll = roll(q, HALF), roll(k, HALF), roll(v, HALF)
        kv = [jnp.where(low, k, v_roll), jnp.where(low, k_roll, v)]
        q_pair = [
            jnp.where(low, q[:32], q_roll[32:64]),
            jnp.where(low, q_roll[:32], q[32:64]),
        ]
        q_last = [q[64:], q_roll[64:]]
        for a in range(2):
            for b in range(2):
                last = jnp.where(low, q_last[a], sizes[a][b])
                out_ref[h * GROUPS + 2 * a + b] = jnp.concatenate(
                    [kv[b], q_pair[a], last], axis=0
                ).astype(jnp.bfloat16)


def attend_kernel(
    got_ref,
    out_ref,
    offs_v,
    offs,
    k_t,
    v_t,
    q_t,
    keys,
    vals,
    queries,
    scores,
    probs,
    done_t,
    sem,
):
    lane = lax.broadcasted_iota(jnp.int32, (1, BLK), 1)
    low = lane < HALF

    row = lax.broadcasted_iota(jnp.int32, (144, DEVICES * 16), 0)
    col = lax.broadcasted_iota(jnp.int32, (144, DEVICES * 16), 1)
    is_q = row >= 72
    index = jnp.where(is_q, row - 72, row)
    line = jnp.where(is_q, 10, 9)
    before = ((col & 15) == line) & ((col >> 4) < index)
    tail = got_ref[:, IN_ROWS - 16 :, :].reshape(DEVICES * 16, BLK)
    offs_v[...] = jnp.dot(
        jnp.where(before, 1.0, 0.0).astype(jnp.bfloat16), tail, preferred_element_type=jnp.float32
    ).astype(jnp.int32)
    copy = pltpu.make_async_copy(offs_v, offs, sem)
    copy.start()
    copy.wait()

    def put(dst, tile, first, last, moved, keep):
        dst[tile, first:last, :] = jnp.where(keep, moved, dst[tile, first:last, :])
        dst[tile + 1, first:last, :] = moved

    k_t[0] = jnp.zeros_like(k_t[0])
    v_t[0] = jnp.zeros_like(v_t[0])
    q_t[0] = jnp.zeros_like(q_t[0])

    def pack(b, _):
        k_at = offs[b, HALF]
        q_at = offs[72 + b, HALF]
        k_tile, k_off = k_at >> 7, k_at & 127
        q_tile, q_off = q_at >> 7, q_at & 127
        message = got_ref[b].astype(jnp.float32)
        keep_k, keep_q = lane >= k_off, lane >= q_off
        k_over, q_over = (k_off + HALF) & 127, (q_off + HALF) & 127
        put(k_t, k_tile, 0, HD, roll(message[:HD], k_off), keep_k)
        put(v_t, k_tile, 0, HD, roll(message[:HD], k_over), keep_k)
        put(k_t, k_tile, HD, AUG, roll(message[104:], k_over), keep_k)
        put(q_t, q_tile, 0, 32, roll(message[HD:104], q_off), keep_q)
        put(q_t, q_tile, 32, 64, roll(message[HD:104], q_over), keep_q)
        put(q_t, q_tile, 64, HD, roll(message[104:], q_off), keep_q)
        return 0

    lax.fori_loop(0, DEVICES, pack, 0, unroll=2)

    total = offs[64, HALF]
    line8 = lax.broadcasted_iota(jnp.int32, (8, BLK), 0)
    zeros = jnp.zeros((BLK - AUG, BLK), jnp.float32)
    ones2 = jnp.where(line8 < 2, 1.0, 0.0)
    ones1 = jnp.where(line8 < 1, 1.0, 0.0)
    written = TILES - 1
    for t in range(TILES):
        if t < written:
            members = jnp.broadcast_to(k_t[t, HD : HD + 1, :], (8, BLK))
            bias = jnp.log(jnp.maximum(members, 1.0)) * (1.0 / INVERSE)
            bias = jnp.where(lane + t * BLK < total, bias, -1e30)
            high = bias.astype(jnp.bfloat16).astype(jnp.float32)
            rest = jnp.where(line8 == 0, high, jnp.where(line8 == 1, bias - high, 0.0))
            k_tile, v_tile, q_tile = k_t[t, :HD, :], v_t[t, :HD, :], q_t[t, :HD, :]
        else:
            rest = jnp.where(line8 == 0, -1e30, 0.0)
            k_tile = v_tile = q_tile = jnp.zeros((HD, BLK), jnp.float32)
        cols = slice(t * BLK, (t + 1) * BLK)
        keys[cols, :] = jnp.concatenate([k_tile, rest, zeros], axis=0).T.astype(jnp.bfloat16)
        vals[:, cols] = jnp.concatenate([v_tile, ones1], axis=0).astype(jnp.bfloat16)
        queries[t // 2, :, (t % 2) * BLK : (t % 2 + 1) * BLK] = jnp.concatenate(
            [q_tile, ones2, zeros], axis=0
        ).astype(jnp.bfloat16)

    def attend(i, _):
        s = jnp.dot(keys[...], queries[i], preferred_element_type=jnp.float32)
        scores[...] = s
        top = jnp.max(s, axis=0, keepdims=True)
        probs[...] = jnp.exp2((scores[...] - top) * (INVERSE * LOG2E)).astype(jnp.bfloat16)
        o = jnp.dot(vals[...], probs[...], preferred_element_type=jnp.float32)
        mass = o[HD : HD + 1]
        lse = jnp.broadcast_to(top * INVERSE + jnp.log(mass), (8, WIDE))
        high = lse.astype(jnp.bfloat16).astype(jnp.float32)
        line = lax.broadcasted_iota(jnp.int32, (8, WIDE), 0)
        stats = jnp.where(line == 0, high, jnp.where(line == 1, lse - high, 0.0))
        o = jnp.concatenate([o[:HD] * (1.0 / mass), stats], axis=0)
        done_t[2 * i] = o[:, :BLK]
        done_t[2 * i + 1] = o[:, BLK:]
        return 0

    lax.fori_loop(0, TILES // 2, attend, 0)

    def unpack(b, _):
        at = offs[72 + b, HALF]
        tile, off = at >> 7, at & 127
        both = jnp.where(lane >= off, done_t[tile], done_t[tile + 1])
        first = roll(both[:OUT_ROWS], (BLK - off) & 127)
        second = roll(both[OUT_ROWS:], (BLK + HALF - off) & 127)
        out_ref[b] = jnp.where(low, first, second).astype(jnp.bfloat16)
        return 0

    lax.fori_loop(0, DEVICES, unpack, 0, unroll=2)


def post_kernel(got_ref, slots_ref, tokens_ref, gate_ref, w_ref, out_ref, att_t):
    low = lax.broadcasted_iota(jnp.int32, (1, BLK), 1) < HALF
    for h in range(HEADS):
        halves = []
        for a in range(2):
            parts = [got_ref[h * GROUPS + 2 * a + b].astype(jnp.float32) for b in range(2)]
            lse = [p[32:33] + p[33:34] for p in parts]
            gap = jnp.broadcast_to(lse[1] - lse[0], (8, BLK))
            gap = jnp.where(low, roll(gap, HALF), gap)[:1]
            share = 1.0 / (1.0 + jnp.exp(gap))
            halves.append(parts[0] * share + parts[1] * (1.0 - share))
        x, y = halves
        upper = jnp.where(low, x, roll(y, HALF))
        lower = jnp.where(low, roll(x, HALF), y)
        att_t[h * HD : (h + 1) * HD, :] = jnp.concatenate(
            [upper, lower[: HD - OUT_ROWS]], axis=0
        )
    place = jnp.broadcast_to(place_of(slots_ref[...]), (BLK, BLK))
    row_id = lax.broadcasted_iota(jnp.int32, (BLK, BLK), 0)
    hot = jnp.where(place == row_id, 1.0, 0.0).T.astype(jnp.bfloat16)
    rows = lax.dot_general(
        hot,
        att_t[...].astype(jnp.bfloat16),
        (((1,), (1,)), ((), ())),
        preferred_element_type=jnp.float32,
    ).astype(jnp.bfloat16)
    branch = jnp.dot(rows, w_ref[...], preferred_element_type=jnp.float32)
    out_ref[...] = (tokens_ref[...].astype(jnp.float32) + gate_ref[...] * branch).astype(
        jnp.bfloat16
    )


def vmem():
    return pl.BlockSpec(memory_space=pltpu.VMEM)


def body(tokens, slots, counts, shift, scale, gate, w_qkv, w_out):
    slots = slots.reshape(1, BLK)
    sent = pl.pallas_call(
        pre_kernel,
        out_shape=jax.ShapeDtypeStruct((DEVICES, IN_ROWS, BLK), jnp.bfloat16),
        in_specs=[
            pl.BlockSpec(memory_space=pltpu.SMEM),
            vmem(),
            vmem(),
            vmem(),
            vmem(),
            pl.BlockSpec(memory_space=pl.ANY),
        ],
        out_specs=vmem(),
        scratch_shapes=[
            pltpu.VMEM((W_CHUNKS, D, W_CHUNK), jnp.bfloat16),
            pltpu.VMEM((3 * D, BLK), jnp.float32),
            pltpu.SemaphoreType.DMA((W_CHUNKS,)),
        ],
        compiler_params=pltpu.CompilerParams(vmem_limit_bytes=VMEM),
        name="merge_norm_qkv",
    )(counts, slots, tokens, shift.reshape(1, D), scale.reshape(1, D), w_qkv)
    got = lax.all_to_all(sent, "patch", 0, 0, tiled=True)
    back = pl.pallas_call(
        attend_kernel,
        out_shape=jax.ShapeDtypeStruct((DEVICES, OUT_ROWS, BLK), jnp.bfloat16),
        in_specs=[vmem()],
        out_specs=vmem(),
        scratch_shapes=[
            pltpu.VMEM((144, BLK), jnp.int32),
            pltpu.SMEM((144, BLK), jnp.int32),
            pltpu.VMEM((TILES, AUG, BLK), jnp.float32),
            pltpu.VMEM((TILES, HD, BLK), jnp.float32),
            pltpu.VMEM((TILES, HD, BLK), jnp.float32),
            pltpu.VMEM((COLUMNS, BLK), jnp.bfloat16),
            pltpu.VMEM((AUG, COLUMNS), jnp.bfloat16),
            pltpu.VMEM((TILES // 2, BLK, WIDE), jnp.bfloat16),
            pltpu.VMEM((COLUMNS, WIDE), jnp.float32),
            pltpu.VMEM((COLUMNS, WIDE), jnp.bfloat16),
            pltpu.VMEM((TILES, AUG, BLK), jnp.float32),
            pltpu.SemaphoreType.DMA,
        ],
        compiler_params=pltpu.CompilerParams(vmem_limit_bytes=VMEM),
        name="attend_head",
    )(got)
    returned = lax.all_to_all(back, "patch", 0, 0, tiled=True)
    return pl.pallas_call(
        post_kernel,
        out_shape=jax.ShapeDtypeStruct((BLK, D), jnp.bfloat16),
        in_specs=[vmem()] * 5,
        out_specs=vmem(),
        scratch_shapes=[pltpu.VMEM((D, BLK), jnp.float32)],
        compiler_params=pltpu.CompilerParams(vmem_limit_bytes=VMEM),
        name="combine_project",
    )(returned, slots, tokens, gate.reshape(1, D), w_out)


def solution(mesh):
    split = ("batch", "patch")
    return jax.shard_map(
        body,
        mesh=mesh,
        in_specs=(P(split, None), P(split), P(split), P(), P(), P(), P(), P()),
        out_specs=P(split, None),
        check_vma=False,
    )
```

```python
import jax
import jax.numpy as jnp
from jax import lax
from jax.experimental import pallas as pl
from jax.experimental.pallas import tpu as pltpu
from jax.sharding import PartitionSpec as P

D = 1152
HEADS = 16
HD = 72
BLK = 128
HALF = BLK // 2
DEVICES = 64
GROUPS = DEVICES // HEADS

IN_ROWS = 112
OUT_ROWS = 40
AUG = 80
TILES = 22
WIDE = 2 * BLK
COLUMNS = (TILES - 1) * BLK
Q_ROWS = 288
Q_TILES = 9
W_CHUNK = 384
W_CHUNKS = 3 * D // W_CHUNK
VMEM = 56 * 1024 * 1024

INVERSE = 1.0 / HD**0.5
LOG2E = 1.4426950408889634


def place_of(slots):
    return (slots & 1) * HALF + (slots >> 1)


def roll(x, shift):
    return pltpu.roll(x, shift, 1)


def pre_kernel(
    slots_ref, tokens_ref, shift_ref, scale_ref, w_ref, out_ref, w_buf, qkv_t, sems
):
    copies = [
        pltpu.make_async_copy(
            w_ref.at[:, pl.ds(c * W_CHUNK, W_CHUNK)], w_buf.at[c], sems.at[c]
        )
        for c in range(W_CHUNKS)
    ]
    for copy in copies:
        copy.start()
    place = jnp.broadcast_to(place_of(slots_ref[...]), (BLK, BLK))
    row_id = lax.broadcasted_iota(jnp.int32, (BLK, BLK), 0)
    hot = jnp.where(place == row_id, 1.0, 0.0)
    members = jnp.sum(hot, axis=1, keepdims=True)
    sums = jnp.dot(hot.astype(jnp.bfloat16), tokens_ref[...], preferred_element_type=jnp.float32)
    values = (sums / jnp.maximum(members, 1.0)).astype(jnp.bfloat16).astype(jnp.float32)
    center = jnp.mean(values, axis=-1, keepdims=True)
    off = values - center
    spread = jnp.mean(off * off, axis=-1, keepdims=True)
    normed = (off * lax.rsqrt(spread + 1e-06) * (1.0 + scale_ref[...]) + shift_ref[...]).astype(
        jnp.bfloat16
    )
    for c in range(W_CHUNKS):
        copies[c].wait()
        part = jnp.dot(normed, w_buf[c], preferred_element_type=jnp.float32)
        for t in range(W_CHUNK // BLK):
            at = c * W_CHUNK + t * BLK
            qkv_t[at : at + BLK, :] = part[:, t * BLK : (t + 1) * BLK].T

    members_row = jnp.sum(hot.T, axis=0, keepdims=True)
    low = lax.broadcasted_iota(jnp.int32, (1, BLK), 1) < HALF
    line = lax.broadcasted_iota(jnp.int32, (8, BLK), 0)
    alive = jnp.where(members_row > 0.0, 1.0, 0.0)
    live = [
        jnp.sum(jnp.where(low == even, alive, 0.0), axis=1, keepdims=True) for even in (True, False)
    ]
    sizes_of = [roll(jnp.broadcast_to(members_row, (8, BLK)), HALF)]
    sizes_of.append(jnp.broadcast_to(members_row, (8, BLK)))
    sizes = [
        [
            jnp.where(
                line == 0,
                sizes_of[b],
                jnp.where(line == 1, live[b], jnp.where(line == 2, live[a], 0.0)),
            )
            for b in range(2)
        ]
        for a in range(2)
    ]
    for h in range(HEADS):
        q = qkv_t[h * HD : (h + 1) * HD, :]
        k = qkv_t[D + h * HD : D + (h + 1) * HD, :]
        v = qkv_t[2 * D + h * HD : 2 * D + (h + 1) * HD, :]
        q_roll, k_roll, v_roll = roll(q, HALF), roll(k, HALF), roll(v, HALF)
        kv = [jnp.where(low, k, v_roll), jnp.where(low, k_roll, v)]
        q_pair = [
            jnp.where(low, q[:32], q_roll[32:64]),
            jnp.where(low, q_roll[:32], q[32:64]),
        ]
        q_last = [q[64:], q_roll[64:]]
        for a in range(2):
            for b in range(2):
                last = jnp.where(low, q_last[a], sizes[a][b])
                out_ref[h * GROUPS + 2 * a + b] = jnp.concatenate(
                    [kv[b], q_pair[a], last], axis=0
                ).astype(jnp.bfloat16)


def attend_kernel(
    got_ref,
    out_ref,
    offs_v,
    offs,
    k_t,
    v_t,
    q_t,
    keys,
    vals,
    queries,
    scores_a,
    scores_b,
    top_a,
    top_b,
    done,
    done_t,
    sem,
):
    lane = lax.broadcasted_iota(jnp.int32, (1, BLK), 1)
    low = lane < HALF

    row = lax.broadcasted_iota(jnp.int32, (144, DEVICES * 16), 0)
    col = lax.broadcasted_iota(jnp.int32, (144, DEVICES * 16), 1)
    is_q = row >= 72
    index = jnp.where(is_q, row - 72, row)
    line = jnp.where(is_q, 10, 9)
    before = ((col & 15) == line) & ((col >> 4) < index)
    tail = got_ref[:, IN_ROWS - 16 :, :].reshape(DEVICES * 16, BLK)
    offs_v[...] = jnp.dot(
        jnp.where(before, 1.0, 0.0).astype(jnp.bfloat16), tail, preferred_element_type=jnp.float32
    ).astype(jnp.int32)
    copy = pltpu.make_async_copy(offs_v, offs, sem)
    copy.start()
    copy.wait()

    def put(dst, tile, first, last, moved, keep):
        dst[tile, first:last, :] = jnp.where(keep, moved, dst[tile, first:last, :])
        dst[tile + 1, first:last, :] = moved

    k_t[0] = jnp.zeros_like(k_t[0])
    v_t[0] = jnp.zeros_like(v_t[0])
    q_t[0] = jnp.zeros_like(q_t[0])

    def pack(b, _):
        k_at = offs[b, HALF]
        q_at = offs[72 + b, HALF]
        k_tile, k_off = k_at >> 7, k_at & 127
        q_tile, q_off = q_at >> 7, q_at & 127
        message = got_ref[b].astype(jnp.float32)
        keep_k, keep_q = lane >= k_off, lane >= q_off
        k_over, q_over = (k_off + HALF) & 127, (q_off + HALF) & 127
        put(k_t, k_tile, 0, HD, roll(message[:HD], k_off), keep_k)
        put(v_t, k_tile, 0, HD, roll(message[:HD], k_over), keep_k)
        put(k_t, k_tile, HD, AUG, roll(message[104:], k_over), keep_k)
        put(q_t, q_tile, 0, 32, roll(message[HD:104], q_off), keep_q)
        put(q_t, q_tile, 32, 64, roll(message[HD:104], q_over), keep_q)
        put(q_t, q_tile, 64, HD, roll(message[104:], q_off), keep_q)
        return 0

    lax.fori_loop(0, DEVICES, pack, 0, unroll=8)

    total = offs[64, HALF]
    line8 = lax.broadcasted_iota(jnp.int32, (8, BLK), 0)
    zeros = jnp.zeros((BLK - AUG, BLK), jnp.float32)
    ones2 = jnp.where(line8 < 2, 1.0, 0.0)
    ones1 = jnp.where(line8 < 1, 1.0, 0.0)
    for t in range(TILES - 1):
        members = jnp.broadcast_to(k_t[t, HD : HD + 1, :], (8, BLK))
        bias = jnp.log(jnp.maximum(members, 1.0)) * (1.0 / INVERSE)
        bias = jnp.where(lane + t * BLK < total, bias, -1e30)
        high = bias.astype(jnp.bfloat16).astype(jnp.float32)
        rest = jnp.where(line8 == 0, high, jnp.where(line8 == 1, bias - high, 0.0))
        k_tile, v_tile, q_tile = k_t[t, :HD, :], v_t[t, :HD, :], q_t[t, :HD, :]
        cols = slice(t * BLK, (t + 1) * BLK)
        keys[:, cols] = jnp.concatenate([k_tile, rest, zeros], axis=0).astype(jnp.bfloat16)
        vals[cols, :] = jnp.concatenate([v_tile, ones1, zeros], axis=0).T.astype(jnp.bfloat16)
        queries[cols, :] = jnp.concatenate([q_tile, ones2, zeros], axis=0).T.astype(jnp.bfloat16)

    chunks = [slice(at, min(at + WIDE, COLUMNS)) for at in range(0, COLUMNS, WIDE)]

    def rows_of(i):
        return pl.ds(pl.multiple_of(i * Q_ROWS, 16), Q_ROWS)

    def fold(s, best):
        for t in range(s.shape[1] // BLK):
            part = s[:, t * BLK : (t + 1) * BLK]
            best = part if best is None else jnp.maximum(best, part)
        return best

    def step(i, scores, top, ahead_scores, ahead_top):
        best = None
        o = None
        q = queries[rows_of(i + 1), :] if ahead_scores is not None else None
        for c in chunks:
            if ahead_scores is not None:
                s = jnp.dot(q, keys[:, c], preferred_element_type=jnp.float32)
                ahead_scores[:, c] = s
                best = fold(s, best)
            if scores is not None:
                n = (c.stop - c.start) // BLK
                p = [
                    jnp.exp2(
                        (scores[:, c.start + t * BLK : c.start + (t + 1) * BLK] - top[...])
                        * (INVERSE * LOG2E)
                    ).astype(jnp.bfloat16)
                    for t in range(n)
                ]
                p = jnp.concatenate(p, axis=1)
                part = jnp.dot(p, vals[c, :], preferred_element_type=jnp.float32)
                o = part if o is None else o + part
        if ahead_scores is not None:
            ahead_top[...] = jnp.broadcast_to(
                jnp.max(best, axis=1, keepdims=True), (Q_ROWS, BLK)
            )
        if scores is not None:
            mass = jnp.broadcast_to(o[:, HD : HD + 1], (Q_ROWS, BLK))
            lse = top[...] * INVERSE + jnp.log(mass)
            high = lse.astype(jnp.bfloat16).astype(jnp.float32)
            done[rows_of(i), :] = jnp.where(
                lane < HD, o / mass, jnp.where(lane == HD, high, lse - high)
            )

    def two(i, _):
        step(2 * i, scores_a, top_a, scores_b, top_b)
        step(2 * i + 1, scores_b, top_b, scores_a, top_a)
        return 0

    step(-1, None, None, scores_a, top_a)
    pairs = (Q_TILES - 1) // 2
    lax.fori_loop(0, pairs, two, 0)
    if Q_TILES % 2 == 0:
        step(Q_TILES - 2, scores_a, top_a, scores_b, top_b)
        step(Q_TILES - 1, scores_b, top_b, None, None)
    else:
        step(Q_TILES - 1, scores_a, top_a, None, None)

    for t in range(TILES - 1):
        last = min((t + 1) * BLK, Q_TILES * Q_ROWS)
        tile = done[t * BLK : last, :]
        if last < (t + 1) * BLK:
            tile = jnp.concatenate(
                [tile, jnp.zeros(((t + 1) * BLK - last, BLK), jnp.float32)], axis=0
            )
        done_t[t] = tile.T[:AUG]
    done_t[TILES - 1] = jnp.zeros((AUG, BLK), jnp.float32)

    def unpack(b, _):
        at = offs[72 + b, HALF]
        tile, off = at >> 7, at & 127
        both = jnp.where(lane >= off, done_t[tile], done_t[tile + 1])
        first = roll(both[:OUT_ROWS], (BLK - off) & 127)
        second = roll(both[OUT_ROWS:], (BLK + HALF - off) & 127)
        out_ref[b] = jnp.where(low, first, second).astype(jnp.bfloat16)
        return 0

    lax.fori_loop(0, DEVICES, unpack, 0, unroll=8)


def post_kernel(got_ref, slots_ref, tokens_ref, gate_ref, w_ref, out_ref, att_t, w_buf, sem):
    copy = pltpu.make_async_copy(w_ref, w_buf, sem)
    copy.start()
    low = lax.broadcasted_iota(jnp.int32, (1, BLK), 1) < HALF
    for h in range(HEADS):
        halves = []
        for a in range(2):
            parts = [got_ref[h * GROUPS + 2 * a + b].astype(jnp.float32) for b in range(2)]
            lse = [p[32:33] + p[33:34] for p in parts]
            gap = jnp.broadcast_to(lse[1] - lse[0], (8, BLK))
            gap = jnp.where(low, roll(gap, HALF), gap)[:1]
            share = 1.0 / (1.0 + jnp.exp(gap))
            halves.append(parts[0] * share + parts[1] * (1.0 - share))
        x, y = halves
        upper = jnp.where(low, x, roll(y, HALF))
        lower = jnp.where(low, roll(x, HALF), y)
        att_t[h * HD : (h + 1) * HD, :] = jnp.concatenate(
            [upper, lower[: HD - OUT_ROWS]], axis=0
        )
    place = jnp.broadcast_to(place_of(slots_ref[...]), (BLK, BLK))
    row_id = lax.broadcasted_iota(jnp.int32, (BLK, BLK), 0)
    hot = jnp.where(place == row_id, 1.0, 0.0).T.astype(jnp.bfloat16)
    rows = lax.dot_general(
        hot,
        att_t[...].astype(jnp.bfloat16),
        (((1,), (1,)), ((), ())),
        preferred_element_type=jnp.float32,
    ).astype(jnp.bfloat16)
    copy.wait()
    branch = jnp.dot(rows, w_buf[...], preferred_element_type=jnp.float32)
    out_ref[...] = (tokens_ref[...].astype(jnp.float32) + gate_ref[...] * branch).astype(
        jnp.bfloat16
    )


def vmem():
    return pl.BlockSpec(memory_space=pltpu.VMEM)


def pre(slots, tokens, shift, scale, w_qkv):
    return pl.pallas_call(
        pre_kernel,
        out_shape=jax.ShapeDtypeStruct((DEVICES, IN_ROWS, BLK), jnp.bfloat16),
        in_specs=[
            vmem(),
            vmem(),
            vmem(),
            vmem(),
            pl.BlockSpec(memory_space=pl.ANY),
        ],
        out_specs=vmem(),
        scratch_shapes=[
            pltpu.VMEM((W_CHUNKS, D, W_CHUNK), jnp.bfloat16),
            pltpu.VMEM((3 * D, BLK), jnp.float32),
            pltpu.SemaphoreType.DMA((W_CHUNKS,)),
        ],
        compiler_params=pltpu.CompilerParams(vmem_limit_bytes=VMEM),
        name="merge_norm_qkv",
    )(slots, tokens, shift, scale, w_qkv)


def attend(got):
    return pl.pallas_call(
        attend_kernel,
        out_shape=jax.ShapeDtypeStruct((DEVICES, OUT_ROWS, BLK), jnp.bfloat16),
        in_specs=[vmem()],
        out_specs=vmem(),
        scratch_shapes=[
            pltpu.VMEM((144, BLK), jnp.int32),
            pltpu.SMEM((144, BLK), jnp.int32),
            pltpu.VMEM((TILES, AUG, BLK), jnp.float32),
            pltpu.VMEM((TILES, HD, BLK), jnp.float32),
            pltpu.VMEM((TILES, HD, BLK), jnp.float32),
            pltpu.VMEM((BLK, COLUMNS), jnp.bfloat16),
            pltpu.VMEM((COLUMNS, BLK), jnp.bfloat16),
            pltpu.VMEM((COLUMNS, BLK), jnp.bfloat16),
            pltpu.VMEM((Q_ROWS, COLUMNS), jnp.float32),
            pltpu.VMEM((Q_ROWS, COLUMNS), jnp.float32),
            pltpu.VMEM((Q_ROWS, BLK), jnp.float32),
            pltpu.VMEM((Q_ROWS, BLK), jnp.float32),
            pltpu.VMEM((Q_ROWS * Q_TILES, BLK), jnp.float32),
            pltpu.VMEM((TILES, AUG, BLK), jnp.float32),
            pltpu.SemaphoreType.DMA,
        ],
        compiler_params=pltpu.CompilerParams(vmem_limit_bytes=VMEM),
        name="attend_head",
    )(got)


def post(returned, slots, tokens, gate, w_out):
    return pl.pallas_call(
        post_kernel,
        out_shape=jax.ShapeDtypeStruct((BLK, D), jnp.bfloat16),
        in_specs=[vmem()] * 4 + [pl.BlockSpec(memory_space=pl.ANY)],
        out_specs=vmem(),
        scratch_shapes=[
            pltpu.VMEM((D, BLK), jnp.float32),
            pltpu.VMEM((D, D), jnp.bfloat16),
            pltpu.SemaphoreType.DMA,
        ],
        compiler_params=pltpu.CompilerParams(vmem_limit_bytes=VMEM),
        name="combine_project",
    )(returned, slots, tokens, gate, w_out)


def body(tokens, slots, counts, shift, scale, gate, w_qkv, w_out):
    sent = pre(slots, tokens, shift, scale, w_qkv)
    got = lax.all_to_all(sent, "patch", 0, 0, tiled=True)
    back = attend(got)
    returned = lax.all_to_all(back, "patch", 0, 0, tiled=True)
    return post(returned, slots, tokens, gate, w_out)


def solution(mesh):
    split = ("batch", "patch")
    return jax.shard_map(
        body,
        mesh=mesh,
        in_specs=(P(split, None), P(split), P(split), P(), P(), P(), P(), P()),
        out_specs=P(split, None),
        check_vma=False,
    )
```

```python
import jax
import jax.numpy as jnp
from jax import lax
from jax.experimental import pallas as pl
from jax.experimental.pallas import tpu as pltpu
from jax.sharding import PartitionSpec as P

D = 1152
HEADS = 16
HD = 72
BLK = 128
HALF = BLK // 2
DEVICES = 64
GROUPS = DEVICES // HEADS

IN_ROWS = 112
OUT_ROWS = 40
AUG = 80
TILES = 22
CHUNK = 2 * BLK
COLUMNS = (TILES - 1) * BLK
Q_ROWS = 656
PIECES = 4
Q_TILES = 4
EARLY = 64
VMEM = 56 * 1024 * 1024

INVERSE = 1.0 / HD**0.5
LOG2E = 1.4426950408889634


def place_of(slots):
    return (slots & 1) * HALF + (slots >> 1)


def roll(x, shift):
    return pltpu.roll(x, shift, 1)


def pre_kernel(
    slots_ref,
    tokens_ref,
    shift_ref,
    scale_ref,
    w_ref,
    out_ref,
    slots_buf,
    tok_buf,
    shift_buf,
    scale_buf,
    w_buf,
    qkv_t,
    messages,
    in_sems,
    w_sems,
    out_sems,
):
    small = [
        pltpu.make_async_copy(src, dst, in_sems.at[i])
        for i, (src, dst) in enumerate(
            [
                (slots_ref, slots_buf),
                (tokens_ref, tok_buf),
                (shift_ref, shift_buf),
                (scale_ref, scale_buf),
            ]
        )
    ]
    for copy in small:
        copy.start()
    large = [
        pltpu.make_async_copy(w_ref.at[:, pl.ds(part * D, D)], w_buf.at[part], w_sems.at[part])
        for part in (1, 2, 0)
    ]
    for copy in large:
        copy.start()

    small[0].wait()
    place = jnp.broadcast_to(place_of(slots_buf[...]), (BLK, BLK))
    row_id = lax.broadcasted_iota(jnp.int32, (BLK, BLK), 0)
    hot = jnp.where(place == row_id, 1.0, 0.0)
    members = jnp.sum(hot, axis=1, keepdims=True)
    members_row = jnp.sum(hot.T, axis=0, keepdims=True)
    low = lax.broadcasted_iota(jnp.int32, (1, BLK), 1) < HALF
    line = lax.broadcasted_iota(jnp.int32, (8, BLK), 0)
    alive = jnp.where(members_row > 0.0, 1.0, 0.0)
    live = [
        jnp.sum(jnp.where(low == even, alive, 0.0), axis=1, keepdims=True) for even in (True, False)
    ]
    sizes_of = [roll(jnp.broadcast_to(members_row, (8, BLK)), HALF)]
    sizes_of.append(jnp.broadcast_to(members_row, (8, BLK)))
    sizes = [
        [
            jnp.where(
                line == 0,
                sizes_of[b],
                jnp.where(line == 1, live[b], jnp.where(line == 2, live[a], 0.0)),
            )
            for b in range(2)
        ]
        for a in range(2)
    ]

    for copy in small[1:]:
        copy.wait()
    sums = jnp.dot(hot.astype(jnp.bfloat16), tok_buf[...], preferred_element_type=jnp.float32)
    values = (sums / jnp.maximum(members, 1.0)).astype(jnp.bfloat16).astype(jnp.float32)
    center = jnp.mean(values, axis=-1, keepdims=True)
    off = values - center
    spread = jnp.mean(off * off, axis=-1, keepdims=True)
    normed = (off * lax.rsqrt(spread + 1e-06) * (1.0 + scale_buf[...]) + shift_buf[...]).astype(
        jnp.bfloat16
    )

    def project(part):
        out = jnp.dot(normed, w_buf[part], preferred_element_type=jnp.float32)
        for t in range(D // BLK):
            qkv_t[part, t * BLK : (t + 1) * BLK, :] = out[:, t * BLK : (t + 1) * BLK].T

    large[0].wait()
    project(1)
    large[1].wait()
    project(2)
    early = []
    for h in range(HEADS):
        k = qkv_t[1, h * HD : (h + 1) * HD, :]
        v = qkv_t[2, h * HD : (h + 1) * HD, :]
        kv = [jnp.where(low, k, roll(v, HALF)), jnp.where(low, roll(k, HALF), v)]
        early.append([x[EARLY:] for x in kv])
        for a in range(2):
            for b in range(2):
                messages[h * GROUPS + 2 * a + b, :EARLY, :] = kv[b][:EARLY].astype(jnp.bfloat16)
    first = pltpu.make_async_copy(
        messages.at[:, pl.ds(0, EARLY)], out_ref.at[:, pl.ds(0, EARLY)], out_sems.at[0]
    )
    first.start()
    large[2].wait()
    project(0)
    for h in range(HEADS):
        q = qkv_t[0, h * HD : (h + 1) * HD, :]
        q_roll = roll(q, HALF)
        q_pair = [
            jnp.where(low, q[:32], q_roll[32:64]),
            jnp.where(low, q_roll[:32], q[32:64]),
        ]
        q_last = [q[64:], q_roll[64:]]
        for a in range(2):
            for b in range(2):
                last = jnp.where(low, q_last[a], sizes[a][b])
                messages[h * GROUPS + 2 * a + b, EARLY:, :] = jnp.concatenate(
                    [early[h][b], q_pair[a], last], axis=0
                ).astype(jnp.bfloat16)
    second = pltpu.make_async_copy(
        messages.at[:, pl.ds(EARLY, IN_ROWS - EARLY)],
        out_ref.at[:, pl.ds(EARLY, IN_ROWS - EARLY)],
        out_sems.at[1],
    )
    second.start()
    first.wait()
    second.wait()


def attend_kernel(
    got_ref,
    out_ref,
    tail,
    got,
    out,
    offs_v,
    offs,
    k_t,
    v_t,
    q_t,
    keys,
    vals,
    queries,
    scores_a,
    scores_b,
    top_a,
    top_b,
    done,
    done_t,
    sem,
    tail_sem,
    got_sems,
    out_sems,
):
    each = DEVICES // PIECES
    pieces = [pl.ds(i * each, each) for i in range(PIECES)]
    tail_copy = pltpu.make_async_copy(
        got_ref.at[:, pl.ds(IN_ROWS - 16, 16)], tail, tail_sem
    )
    tail_copy.start()
    got_copies = [
        pltpu.make_async_copy(got_ref.at[p], got.at[p], got_sems.at[i])
        for i, p in enumerate(pieces)
    ]
    for copy in got_copies:
        copy.start()
    lane = lax.broadcasted_iota(jnp.int32, (1, BLK), 1)
    low = lane < HALF

    row = lax.broadcasted_iota(jnp.int32, (BLK, DEVICES * 16), 0)
    col = lax.broadcasted_iota(jnp.int32, (BLK, DEVICES * 16), 1)
    tail_copy.wait()
    last_rows = tail[...].reshape(DEVICES * 16, BLK)
    for x in range(2):
        before = (col < row * 16) & ((col & 15) == 9 + x)
        sums = jnp.dot(
            jnp.where(before, 1.0, 0.0).astype(jnp.bfloat16),
            last_rows,
            preferred_element_type=jnp.float32,
        )
        offs_v[8 * x : 8 * x + 8, :] = sums.T[HALF : HALF + 8].astype(jnp.int32)
    copy = pltpu.make_async_copy(offs_v, offs, sem)
    copy.start()
    copy.wait()

    def put(dst, tile, first, last, moved, keep):
        dst[tile, first:last, :] = jnp.where(keep, moved, dst[tile, first:last, :])
        dst[tile + 1, first:last, :] = moved

    k_t[0] = jnp.zeros_like(k_t[0])
    v_t[0] = jnp.zeros_like(v_t[0])
    q_t[0] = jnp.zeros_like(q_t[0])

    def pack(b, _):
        k_at = offs[0, b]
        q_at = offs[8, b]
        k_tile, k_off = k_at >> 7, k_at & 127
        q_tile, q_off = q_at >> 7, q_at & 127
        message = got[b].astype(jnp.float32)
        keep_k, keep_q = lane >= k_off, lane >= q_off
        k_over, q_over = (k_off + HALF) & 127, (q_off + HALF) & 127
        put(k_t, k_tile, 0, HD, roll(message[:HD], k_off), keep_k)
        put(v_t, k_tile, 0, HD, roll(message[:HD], k_over), keep_k)
        put(k_t, k_tile, HD, AUG, roll(message[104:], k_over), keep_k)
        put(q_t, q_tile, 0, 32, roll(message[HD:104], q_off), keep_q)
        put(q_t, q_tile, 32, 64, roll(message[HD:104], q_over), keep_q)
        put(q_t, q_tile, 64, HD, roll(message[104:], q_off), keep_q)
        return 0

    for i in range(PIECES):
        got_copies[i].wait()
        lax.fori_loop(i * each, (i + 1) * each, pack, 0, unroll=each)

    total = offs[0, DEVICES]
    line8 = lax.broadcasted_iota(jnp.int32, (8, BLK), 0)
    zeros = jnp.zeros((BLK - AUG, BLK), jnp.float32)
    ones2 = jnp.where(line8 < 2, 1.0, 0.0)
    ones1 = jnp.where(line8 < 1, 1.0, 0.0)
    for t in range(TILES - 1):
        members = jnp.broadcast_to(k_t[t, HD : HD + 1, :], (8, BLK))
        bias = jnp.log(jnp.maximum(members, 1.0)) * (1.0 / INVERSE)
        bias = jnp.where(lane + t * BLK < total, bias, -1e30)
        high = bias.astype(jnp.bfloat16).astype(jnp.float32)
        rest = jnp.where(line8 == 0, high, jnp.where(line8 == 1, bias - high, 0.0))
        k_tile, v_tile, q_tile = k_t[t, :HD, :], v_t[t, :HD, :], q_t[t, :HD, :]
        cols = slice(t * BLK, (t + 1) * BLK)
        keys[:, cols] = jnp.concatenate([k_tile, rest, zeros], axis=0).astype(jnp.bfloat16)
        vals[cols, :] = jnp.concatenate([v_tile, ones1, zeros], axis=0).T.astype(jnp.bfloat16)
        queries[cols, :] = jnp.concatenate([q_tile, ones2, zeros], axis=0).T.astype(jnp.bfloat16)

    chunks = [slice(at, min(at + CHUNK, COLUMNS)) for at in range(0, COLUMNS, CHUNK)]

    def rows_of(i):
        return pl.ds(pl.multiple_of(i * Q_ROWS, 16), Q_ROWS)

    def fold(s, best):
        for t in range(s.shape[1] // BLK):
            part = s[:, t * BLK : (t + 1) * BLK]
            best = part if best is None else jnp.maximum(best, part)
        return best

    def step(i, scores, top, ahead_scores, ahead_top):
        best = None
        o = None
        q = queries[rows_of(i + 1), :] if ahead_scores is not None else None
        for c in chunks:
            if ahead_scores is not None:
                s = jnp.dot(q, keys[:, c], preferred_element_type=jnp.float32)
                ahead_scores[:, c] = s
                best = fold(s, best)
            if scores is not None:
                n = (c.stop - c.start) // BLK
                p = [
                    jnp.exp2(
                        (scores[:, c.start + t * BLK : c.start + (t + 1) * BLK] - top[...])
                        * (INVERSE * LOG2E)
                    ).astype(jnp.bfloat16)
                    for t in range(n)
                ]
                p = jnp.concatenate(p, axis=1)
                part = jnp.dot(p, vals[c, :], preferred_element_type=jnp.float32)
                o = part if o is None else o + part
        if ahead_scores is not None:
            ahead_top[...] = jnp.broadcast_to(
                jnp.max(best, axis=1, keepdims=True), (Q_ROWS, BLK)
            )
        if scores is not None:
            mass = jnp.broadcast_to(o[:, HD : HD + 1], (Q_ROWS, BLK))
            lse = top[...] * INVERSE + jnp.log(mass)
            high = lse.astype(jnp.bfloat16).astype(jnp.float32)
            done[rows_of(i), :] = jnp.where(
                lane < HD, o / mass, jnp.where(lane == HD, high, lse - high)
            )

    def two(i, _):
        step(2 * i, scores_a, top_a, scores_b, top_b)
        step(2 * i + 1, scores_b, top_b, scores_a, top_a)
        return 0

    step(-1, None, None, scores_a, top_a)
    pairs = (Q_TILES - 1) // 2
    lax.fori_loop(0, pairs, two, 0)
    if Q_TILES % 2 == 0:
        step(Q_TILES - 2, scores_a, top_a, scores_b, top_b)
        step(Q_TILES - 1, scores_b, top_b, None, None)
    else:
        step(Q_TILES - 1, scores_a, top_a, None, None)

    for t in range(TILES - 1):
        last = min((t + 1) * BLK, Q_TILES * Q_ROWS)
        tile = done[t * BLK : last, :]
        if last < (t + 1) * BLK:
            tile = jnp.concatenate(
                [tile, jnp.zeros(((t + 1) * BLK - last, BLK), jnp.float32)], axis=0
            )
        done_t[t] = tile.T[:AUG]
    done_t[TILES - 1] = jnp.zeros((AUG, BLK), jnp.float32)

    def unpack(b, _):
        at = offs[8, b]
        tile, off = at >> 7, at & 127
        both = jnp.where(lane >= off, done_t[tile], done_t[tile + 1])
        first = roll(both[:OUT_ROWS], (BLK - off) & 127)
        second = roll(both[OUT_ROWS:], (BLK + HALF - off) & 127)
        out[b] = jnp.where(low, first, second).astype(jnp.bfloat16)
        return 0

    out_copies = []
    for i, p in enumerate(pieces):
        lax.fori_loop(i * each, (i + 1) * each, unpack, 0, unroll=each)
        out_copies.append(pltpu.make_async_copy(out.at[p], out_ref.at[p], out_sems.at[i]))
        out_copies[i].start()
    for copy in out_copies:
        copy.wait()


def post_kernel(
    got_ref,
    slots_ref,
    tokens_ref,
    gate_ref,
    w_ref,
    out_ref,
    got,
    slots_buf,
    tok_buf,
    gate_buf,
    w_buf,
    att_t,
    got_sems,
    in_sems,
):
    step = DEVICES // PIECES
    got_copies = [
        pltpu.make_async_copy(
            got_ref.at[pl.ds(i * step, step)], got.at[pl.ds(i * step, step)], got_sems.at[i]
        )
        for i in range(PIECES)
    ]
    others = [
        pltpu.make_async_copy(src, dst, in_sems.at[i])
        for i, (src, dst) in enumerate(
            [
                (slots_ref, slots_buf),
                (w_ref, w_buf),
                (tokens_ref, tok_buf),
                (gate_ref, gate_buf),
            ]
        )
    ]
    for copy in got_copies + others:
        copy.start()
    others[0].wait()
    place = jnp.broadcast_to(place_of(slots_buf[...]), (BLK, BLK))
    row_id = lax.broadcasted_iota(jnp.int32, (BLK, BLK), 0)
    hot = jnp.where(place == row_id, 1.0, 0.0).T.astype(jnp.bfloat16)
    low = lax.broadcasted_iota(jnp.int32, (1, BLK), 1) < HALF
    for h in range(HEADS):
        if h % (HEADS // PIECES) == 0:
            got_copies[h // (HEADS // PIECES)].wait()
        halves = []
        for a in range(2):
            parts = [got[h * GROUPS + 2 * a + b].astype(jnp.float32) for b in range(2)]
            lse = [p[32:33] + p[33:34] for p in parts]
            gap = jnp.broadcast_to(lse[1] - lse[0], (8, BLK))
            gap = jnp.where(low, roll(gap, HALF), gap)[:1]
            share = 1.0 / (1.0 + jnp.exp(gap))
            halves.append(parts[0] * share + parts[1] * (1.0 - share))
        x, y = halves
        upper = jnp.where(low, x, roll(y, HALF))
        lower = jnp.where(low, roll(x, HALF), y)
        att_t[h * HD : (h + 1) * HD, :] = jnp.concatenate(
            [upper, lower[: HD - OUT_ROWS]], axis=0
        )
    rows = lax.dot_general(
        hot,
        att_t[...].astype(jnp.bfloat16),
        (((1,), (1,)), ((), ())),
        preferred_element_type=jnp.float32,
    ).astype(jnp.bfloat16)
    for copy in others[1:]:
        copy.wait()
    branch = jnp.dot(rows, w_buf[...], preferred_element_type=jnp.float32)
    out_ref[...] = (tok_buf[...].astype(jnp.float32) + gate_buf[...] * branch).astype(jnp.bfloat16)


def vmem():
    return pl.BlockSpec(memory_space=pltpu.VMEM)


def hbm():
    return pl.BlockSpec(memory_space=pl.ANY)


def pre(slots, tokens, shift, scale, w_qkv):
    return pl.pallas_call(
        pre_kernel,
        out_shape=jax.ShapeDtypeStruct((DEVICES, IN_ROWS, BLK), jnp.bfloat16),
        in_specs=[hbm()] * 5,
        out_specs=hbm(),
        scratch_shapes=[
            pltpu.VMEM((BLK,), jnp.int32),
            pltpu.VMEM((BLK, D), jnp.bfloat16),
            pltpu.VMEM((D,), jnp.float32),
            pltpu.VMEM((D,), jnp.float32),
            pltpu.VMEM((3, D, D), jnp.bfloat16),
            pltpu.VMEM((3, D, BLK), jnp.float32),
            pltpu.VMEM((DEVICES, IN_ROWS, BLK), jnp.bfloat16),
            pltpu.SemaphoreType.DMA((4,)),
            pltpu.SemaphoreType.DMA((3,)),
            pltpu.SemaphoreType.DMA((2,)),
        ],
        compiler_params=pltpu.CompilerParams(vmem_limit_bytes=VMEM),
        name="merge_norm_qkv",
    )(slots, tokens, shift, scale, w_qkv)


def attend(got):
    return pl.pallas_call(
        attend_kernel,
        out_shape=jax.ShapeDtypeStruct((DEVICES, OUT_ROWS, BLK), jnp.bfloat16),
        in_specs=[hbm()],
        out_specs=hbm(),
        scratch_shapes=[
            pltpu.VMEM((DEVICES, 16, BLK), jnp.bfloat16),
            pltpu.VMEM((DEVICES, IN_ROWS, BLK), jnp.bfloat16),
            pltpu.VMEM((DEVICES, OUT_ROWS, BLK), jnp.bfloat16),
            pltpu.VMEM((16, BLK), jnp.int32),
            pltpu.SMEM((16, BLK), jnp.int32),
            pltpu.VMEM((TILES, AUG, BLK), jnp.float32),
            pltpu.VMEM((TILES, HD, BLK), jnp.float32),
            pltpu.VMEM((TILES, HD, BLK), jnp.float32),
            pltpu.VMEM((BLK, COLUMNS), jnp.bfloat16),
            pltpu.VMEM((COLUMNS, BLK), jnp.bfloat16),
            pltpu.VMEM((COLUMNS, BLK), jnp.bfloat16),
            pltpu.VMEM((Q_ROWS, COLUMNS), jnp.float32),
            pltpu.VMEM((Q_ROWS, COLUMNS), jnp.float32),
            pltpu.VMEM((Q_ROWS, BLK), jnp.float32),
            pltpu.VMEM((Q_ROWS, BLK), jnp.float32),
            pltpu.VMEM((Q_ROWS * Q_TILES, BLK), jnp.float32),
            pltpu.VMEM((TILES, AUG, BLK), jnp.float32),
            pltpu.SemaphoreType.DMA,
            pltpu.SemaphoreType.DMA,
            pltpu.SemaphoreType.DMA((PIECES,)),
            pltpu.SemaphoreType.DMA((PIECES,)),
        ],
        compiler_params=pltpu.CompilerParams(vmem_limit_bytes=VMEM),
        name="attend_head",
    )(got)


def post(returned, slots, tokens, gate, w_out):
    return pl.pallas_call(
        post_kernel,
        out_shape=jax.ShapeDtypeStruct((BLK, D), jnp.bfloat16),
        in_specs=[hbm()] * 5,
        out_specs=vmem(),
        scratch_shapes=[
            pltpu.VMEM((DEVICES, OUT_ROWS, BLK), jnp.bfloat16),
            pltpu.VMEM((BLK,), jnp.int32),
            pltpu.VMEM((BLK, D), jnp.bfloat16),
            pltpu.VMEM((D,), jnp.float32),
            pltpu.VMEM((D, D), jnp.bfloat16),
            pltpu.VMEM((D, BLK), jnp.float32),
            pltpu.SemaphoreType.DMA((PIECES,)),
            pltpu.SemaphoreType.DMA((4,)),
        ],
        compiler_params=pltpu.CompilerParams(vmem_limit_bytes=VMEM),
        name="combine_project",
    )(returned, slots, tokens, gate, w_out)


def body(tokens, slots, counts, shift, scale, gate, w_qkv, w_out):
    sent = pre(slots, tokens, shift, scale, w_qkv)
    got = lax.all_to_all(sent, "patch", 0, 0, tiled=True)
    back = attend(got)
    returned = lax.all_to_all(back, "patch", 0, 0, tiled=True)
    return post(returned, slots, tokens, gate, w_out)


def solution(mesh):
    split = ("batch", "patch")
    return jax.shard_map(
        body,
        mesh=mesh,
        in_specs=(P(split, None), P(split), P(split), P(), P(), P(), P(), P()),
        out_specs=P(split, None),
        check_vma=False,
    )
```

```python
import jax
import jax.numpy as jnp
from jax import lax
from jax.experimental import pallas as pl
from jax.experimental.pallas import tpu as pltpu
from jax.sharding import PartitionSpec as P

D = 1152
HEADS = 16
HD = 72
BLK = 128
HALF = BLK // 2
DEVICES = 64
GROUPS = DEVICES // HEADS

IN_ROWS = 112
OUT_ROWS = 40
AUG = 80
TILES = 22
CHUNK = 2 * BLK
COLUMNS = (TILES - 1) * BLK
Q_ROWS = 656
PIECES = 4
Q_TILES = 4
EARLY = 64
MIB = 1024 * 1024

INVERSE = 1.0 / HD**0.5
LOG2E = 1.4426950408889634


def place_of(slots):
    return (slots & 1) * HALF + (slots >> 1)


def roll(x, shift):
    return pltpu.roll(x, shift, 1)


def pre_kernel(
    slots_ref,
    tokens_ref,
    shift_ref,
    scale_ref,
    w_ref,
    out_ref,
    slots_buf,
    tok_buf,
    shift_buf,
    scale_buf,
    w_buf,
    qkv_t,
    messages,
    in_sems,
    w_sems,
    out_sems,
):
    small = [
        pltpu.make_async_copy(src, dst, in_sems.at[i])
        for i, (src, dst) in enumerate(
            [
                (slots_ref, slots_buf),
                (tokens_ref, tok_buf),
                (shift_ref, shift_buf),
                (scale_ref, scale_buf),
            ]
        )
    ]
    for copy in small:
        copy.start()
    large = [
        pltpu.make_async_copy(w_ref.at[:, pl.ds(part * D, D)], w_buf.at[part], w_sems.at[part])
        for part in (1, 2, 0)
    ]
    for copy in large:
        copy.start()

    small[0].wait()
    place = jnp.broadcast_to(place_of(slots_buf[...]), (BLK, BLK))
    row_id = lax.broadcasted_iota(jnp.int32, (BLK, BLK), 0)
    hot = jnp.where(place == row_id, 1.0, 0.0)
    members = jnp.sum(hot, axis=1, keepdims=True)
    members_row = jnp.sum(hot.T, axis=0, keepdims=True)
    low = lax.broadcasted_iota(jnp.int32, (1, BLK), 1) < HALF
    line = lax.broadcasted_iota(jnp.int32, (8, BLK), 0)
    alive = jnp.where(members_row > 0.0, 1.0, 0.0)
    live = [
        jnp.sum(jnp.where(low == even, alive, 0.0), axis=1, keepdims=True) for even in (True, False)
    ]
    sizes_of = [roll(jnp.broadcast_to(members_row, (8, BLK)), HALF)]
    sizes_of.append(jnp.broadcast_to(members_row, (8, BLK)))
    sizes = [
        [
            jnp.where(
                line == 0,
                sizes_of[b],
                jnp.where(line == 1, live[b], jnp.where(line == 2, live[a], 0.0)),
            )
            for b in range(2)
        ]
        for a in range(2)
    ]

    for copy in small[1:]:
        copy.wait()
    sums = jnp.dot(hot.astype(jnp.bfloat16), tok_buf[...], preferred_element_type=jnp.float32)
    values = (sums / jnp.maximum(members, 1.0)).astype(jnp.bfloat16).astype(jnp.float32)
    center = jnp.mean(values, axis=-1, keepdims=True)
    off = values - center
    spread = jnp.mean(off * off, axis=-1, keepdims=True)
    normed = (off * lax.rsqrt(spread + 1e-06) * (1.0 + scale_buf[...]) + shift_buf[...]).astype(
        jnp.bfloat16
    )

    def project(part):
        out = jnp.dot(normed, w_buf[part], preferred_element_type=jnp.float32)
        for t in range(D // BLK):
            qkv_t[part, t * BLK : (t + 1) * BLK, :] = out[:, t * BLK : (t + 1) * BLK].T

    large[0].wait()
    project(1)
    large[1].wait()
    project(2)
    early = []
    for h in range(HEADS):
        k = qkv_t[1, h * HD : (h + 1) * HD, :]
        v = qkv_t[2, h * HD : (h + 1) * HD, :]
        kv = [jnp.where(low, k, roll(v, HALF)), jnp.where(low, roll(k, HALF), v)]
        early.append([x[EARLY:] for x in kv])
        for a in range(2):
            for b in range(2):
                messages[h * GROUPS + 2 * a + b, :EARLY, :] = kv[b][:EARLY].astype(jnp.bfloat16)
    first = pltpu.make_async_copy(
        messages.at[:, pl.ds(0, EARLY)], out_ref.at[:, pl.ds(0, EARLY)], out_sems.at[0]
    )
    first.start()
    large[2].wait()
    project(0)
    for h in range(HEADS):
        q = qkv_t[0, h * HD : (h + 1) * HD, :]
        q_roll = roll(q, HALF)
        q_pair = [
            jnp.where(low, q[:32], q_roll[32:64]),
            jnp.where(low, q_roll[:32], q[32:64]),
        ]
        q_last = [q[64:], q_roll[64:]]
        for a in range(2):
            for b in range(2):
                last = jnp.where(low, q_last[a], sizes[a][b])
                messages[h * GROUPS + 2 * a + b, EARLY:, :] = jnp.concatenate(
                    [early[h][b], q_pair[a], last], axis=0
                ).astype(jnp.bfloat16)
    second = pltpu.make_async_copy(
        messages.at[:, pl.ds(EARLY, IN_ROWS - EARLY)],
        out_ref.at[:, pl.ds(EARLY, IN_ROWS - EARLY)],
        out_sems.at[1],
    )
    second.start()
    first.wait()
    second.wait()


def attend_kernel(
    got,
    out,
    offs_v,
    offs,
    k_t,
    v_t,
    q_t,
    keys,
    vals,
    queries,
    scores_a,
    scores_b,
    top_a,
    top_b,
    done,
    done_t,
    sem,
):
    lane = lax.broadcasted_iota(jnp.int32, (1, BLK), 1)
    low = lane < HALF

    row = lax.broadcasted_iota(jnp.int32, (BLK, DEVICES * 16), 0)
    col = lax.broadcasted_iota(jnp.int32, (BLK, DEVICES * 16), 1)
    last_rows = got[:, IN_ROWS - 16 :, :].reshape(DEVICES * 16, BLK)
    for x in range(2):
        before = (col < row * 16) & ((col & 15) == 9 + x)
        sums = jnp.dot(
            jnp.where(before, 1.0, 0.0).astype(jnp.bfloat16),
            last_rows,
            preferred_element_type=jnp.float32,
        )
        offs_v[8 * x : 8 * x + 8, :] = sums.T[HALF : HALF + 8].astype(jnp.int32)
    copy = pltpu.make_async_copy(offs_v, offs, sem)
    copy.start()
    copy.wait()

    def put(dst, tile, first, last, moved, keep):
        dst[tile, first:last, :] = jnp.where(keep, moved, dst[tile, first:last, :])
        dst[tile + 1, first:last, :] = moved

    k_t[0] = jnp.zeros_like(k_t[0])
    v_t[0] = jnp.zeros_like(v_t[0])
    q_t[0] = jnp.zeros_like(q_t[0])

    def pack(b, _):
        k_at = offs[0, b]
        q_at = offs[8, b]
        k_tile, k_off = k_at >> 7, k_at & 127
        q_tile, q_off = q_at >> 7, q_at & 127
        message = got[b].astype(jnp.float32)
        keep_k, keep_q = lane >= k_off, lane >= q_off
        k_over, q_over = (k_off + HALF) & 127, (q_off + HALF) & 127
        put(k_t, k_tile, 0, HD, roll(message[:HD], k_off), keep_k)
        put(v_t, k_tile, 0, HD, roll(message[:HD], k_over), keep_k)
        put(k_t, k_tile, HD, AUG, roll(message[104:], k_over), keep_k)
        put(q_t, q_tile, 0, 32, roll(message[HD:104], q_off), keep_q)
        put(q_t, q_tile, 32, 64, roll(message[HD:104], q_over), keep_q)
        put(q_t, q_tile, 64, HD, roll(message[104:], q_off), keep_q)
        return 0

    lax.fori_loop(0, DEVICES, pack, 0, unroll=16)

    total = offs[0, DEVICES]
    line8 = lax.broadcasted_iota(jnp.int32, (8, BLK), 0)
    zeros = jnp.zeros((BLK - AUG, BLK), jnp.float32)
    ones2 = jnp.where(line8 < 2, 1.0, 0.0)
    ones1 = jnp.where(line8 < 1, 1.0, 0.0)
    for t in range(TILES - 1):
        members = jnp.broadcast_to(k_t[t, HD : HD + 1, :], (8, BLK))
        bias = jnp.log(jnp.maximum(members, 1.0)) * (1.0 / INVERSE)
        bias = jnp.where(lane + t * BLK < total, bias, -1e30)
        high = bias.astype(jnp.bfloat16).astype(jnp.float32)
        rest = jnp.where(line8 == 0, high, jnp.where(line8 == 1, bias - high, 0.0))
        k_tile, v_tile, q_tile = k_t[t, :HD, :], v_t[t, :HD, :], q_t[t, :HD, :]
        cols = slice(t * BLK, (t + 1) * BLK)
        keys[:, cols] = jnp.concatenate([k_tile, rest, zeros], axis=0).astype(jnp.bfloat16)
        vals[cols, :] = jnp.concatenate([v_tile, ones1, zeros], axis=0).T.astype(jnp.bfloat16)
        queries[cols, :] = jnp.concatenate([q_tile, ones2, zeros], axis=0).T.astype(jnp.bfloat16)

    chunks = [slice(at, min(at + CHUNK, COLUMNS)) for at in range(0, COLUMNS, CHUNK)]

    def rows_of(i):
        return pl.ds(pl.multiple_of(i * Q_ROWS, 16), Q_ROWS)

    def fold(s, best):
        for t in range(s.shape[1] // BLK):
            part = s[:, t * BLK : (t + 1) * BLK]
            best = part if best is None else jnp.maximum(best, part)
        return best

    def step(i, scores, top, ahead_scores, ahead_top):
        best = None
        o = None
        q = queries[rows_of(i + 1), :] if ahead_scores is not None else None
        for c in chunks:
            if ahead_scores is not None:
                s = jnp.dot(q, keys[:, c], preferred_element_type=jnp.float32)
                ahead_scores[:, c] = s
                best = fold(s, best)
            if scores is not None:
                n = (c.stop - c.start) // BLK
                p = [
                    jnp.exp2(
                        (scores[:, c.start + t * BLK : c.start + (t + 1) * BLK] - top[...])
                        * (INVERSE * LOG2E)
                    ).astype(jnp.bfloat16)
                    for t in range(n)
                ]
                p = jnp.concatenate(p, axis=1)
                part = jnp.dot(p, vals[c, :], preferred_element_type=jnp.float32)
                o = part if o is None else o + part
        if ahead_scores is not None:
            ahead_top[...] = jnp.broadcast_to(
                jnp.max(best, axis=1, keepdims=True), (Q_ROWS, BLK)
            )
        if scores is not None:
            mass = jnp.broadcast_to(o[:, HD : HD + 1], (Q_ROWS, BLK))
            lse = top[...] * INVERSE + jnp.log(mass)
            high = lse.astype(jnp.bfloat16).astype(jnp.float32)
            done[rows_of(i), :] = jnp.where(
                lane < HD, o / mass, jnp.where(lane == HD, high, lse - high)
            )

    def two(i, _):
        step(2 * i, scores_a, top_a, scores_b, top_b)
        step(2 * i + 1, scores_b, top_b, scores_a, top_a)
        return 0

    step(-1, None, None, scores_a, top_a)
    pairs = (Q_TILES - 1) // 2
    lax.fori_loop(0, pairs, two, 0)
    if Q_TILES % 2 == 0:
        step(Q_TILES - 2, scores_a, top_a, scores_b, top_b)
        step(Q_TILES - 1, scores_b, top_b, None, None)
    else:
        step(Q_TILES - 1, scores_a, top_a, None, None)

    for t in range(TILES - 1):
        last = min((t + 1) * BLK, Q_TILES * Q_ROWS)
        tile = done[t * BLK : last, :]
        if last < (t + 1) * BLK:
            tile = jnp.concatenate(
                [tile, jnp.zeros(((t + 1) * BLK - last, BLK), jnp.float32)], axis=0
            )
        done_t[t] = tile.T[:AUG]
    done_t[TILES - 1] = jnp.zeros((AUG, BLK), jnp.float32)

    def unpack(b, _):
        at = offs[8, b]
        tile, off = at >> 7, at & 127
        both = jnp.where(lane >= off, done_t[tile], done_t[tile + 1])
        first = roll(both[:OUT_ROWS], (BLK - off) & 127)
        second = roll(both[OUT_ROWS:], (BLK + HALF - off) & 127)
        out[b] = jnp.where(low, first, second).astype(jnp.bfloat16)
        return 0

    lax.fori_loop(0, DEVICES, unpack, 0, unroll=16)


def post_kernel(got, slots_ref, tokens_ref, gate_ref, w_ref, out_ref, att_t):
    place = jnp.broadcast_to(place_of(slots_ref[...]), (BLK, BLK))
    row_id = lax.broadcasted_iota(jnp.int32, (BLK, BLK), 0)
    hot = jnp.where(place == row_id, 1.0, 0.0).T.astype(jnp.bfloat16)
    low = lax.broadcasted_iota(jnp.int32, (1, BLK), 1) < HALF
    for h in range(HEADS):
        halves = []
        for a in range(2):
            parts = [got[h * GROUPS + 2 * a + b].astype(jnp.float32) for b in range(2)]
            lse = [p[32:33] + p[33:34] for p in parts]
            gap = jnp.broadcast_to(lse[1] - lse[0], (8, BLK))
            gap = jnp.where(low, roll(gap, HALF), gap)[:1]
            share = 1.0 / (1.0 + jnp.exp(gap))
            halves.append(parts[0] * share + parts[1] * (1.0 - share))
        x, y = halves
        upper = jnp.where(low, x, roll(y, HALF))
        lower = jnp.where(low, roll(x, HALF), y)
        att_t[h * HD : (h + 1) * HD, :] = jnp.concatenate(
            [upper, lower[: HD - OUT_ROWS]], axis=0
        )
    rows = lax.dot_general(
        hot,
        att_t[...].astype(jnp.bfloat16),
        (((1,), (1,)), ((), ())),
        preferred_element_type=jnp.float32,
    ).astype(jnp.bfloat16)
    branch = jnp.dot(rows, w_ref[...], preferred_element_type=jnp.float32)
    out_ref[...] = (tokens_ref[...].astype(jnp.float32) + gate_ref[...] * branch).astype(
        jnp.bfloat16
    )


def vmem():
    return pl.BlockSpec(memory_space=pltpu.VMEM)


def hbm():
    return pl.BlockSpec(memory_space=pl.ANY)


def pre(slots, tokens, shift, scale, w_qkv):
    return pl.pallas_call(
        pre_kernel,
        out_shape=jax.ShapeDtypeStruct((DEVICES, IN_ROWS, BLK), jnp.bfloat16),
        in_specs=[hbm()] * 5,
        out_specs=hbm(),
        scratch_shapes=[
            pltpu.VMEM((BLK,), jnp.int32),
            pltpu.VMEM((BLK, D), jnp.bfloat16),
            pltpu.VMEM((D,), jnp.float32),
            pltpu.VMEM((D,), jnp.float32),
            pltpu.VMEM((3, D, D), jnp.bfloat16),
            pltpu.VMEM((3, D, BLK), jnp.float32),
            pltpu.VMEM((DEVICES, IN_ROWS, BLK), jnp.bfloat16),
            pltpu.SemaphoreType.DMA((4,)),
            pltpu.SemaphoreType.DMA((3,)),
            pltpu.SemaphoreType.DMA((2,)),
        ],
        compiler_params=pltpu.CompilerParams(vmem_limit_bytes=56 * MIB),
        name="merge_norm_qkv",
    )(slots, tokens, shift, scale, w_qkv)


def attend(got):
    return pl.pallas_call(
        attend_kernel,
        out_shape=jax.ShapeDtypeStruct((DEVICES, OUT_ROWS, BLK), jnp.bfloat16),
        in_specs=[vmem()],
        out_specs=vmem(),
        scratch_shapes=[
            pltpu.VMEM((16, BLK), jnp.int32),
            pltpu.SMEM((16, BLK), jnp.int32),
            pltpu.VMEM((TILES, AUG, BLK), jnp.float32),
            pltpu.VMEM((TILES, HD, BLK), jnp.float32),
            pltpu.VMEM((TILES, HD, BLK), jnp.float32),
            pltpu.VMEM((BLK, COLUMNS), jnp.bfloat16),
            pltpu.VMEM((COLUMNS, BLK), jnp.bfloat16),
            pltpu.VMEM((COLUMNS, BLK), jnp.bfloat16),
            pltpu.VMEM((Q_ROWS, COLUMNS), jnp.float32),
            pltpu.VMEM((Q_ROWS, COLUMNS), jnp.float32),
            pltpu.VMEM((Q_ROWS, BLK), jnp.float32),
            pltpu.VMEM((Q_ROWS, BLK), jnp.float32),
            pltpu.VMEM((Q_ROWS * Q_TILES, BLK), jnp.float32),
            pltpu.VMEM((TILES, AUG, BLK), jnp.float32),
            pltpu.SemaphoreType.DMA,
        ],
        compiler_params=pltpu.CompilerParams(vmem_limit_bytes=30 * MIB),
        name="attend_head",
    )(got)


def post(returned, slots, tokens, gate, w_out):
    return pl.pallas_call(
        post_kernel,
        out_shape=jax.ShapeDtypeStruct((BLK, D), jnp.bfloat16),
        in_specs=[vmem()] * 5,
        out_specs=vmem(),
        scratch_shapes=[pltpu.VMEM((D, BLK), jnp.float32)],
        compiler_params=pltpu.CompilerParams(vmem_limit_bytes=8 * MIB),
        name="combine_project",
    )(returned, slots, tokens, gate, w_out)


def body(tokens, slots, counts, shift, scale, gate, w_qkv, w_out):
    sent = pre(slots, tokens, shift, scale, w_qkv)
    got = lax.all_to_all(sent, "patch", 0, 0, tiled=True)
    back = attend(got)
    returned = lax.all_to_all(back, "patch", 0, 0, tiled=True)
    return post(returned, slots, tokens, gate, w_out)


def solution(mesh):
    split = ("batch", "patch")
    return jax.shard_map(
        body,
        mesh=mesh,
        in_specs=(P(split, None), P(split), P(split), P(), P(), P(), P(), P()),
        out_specs=P(split, None),
        check_vma=False,
    )
```

```python
import functools

import jax
import jax.numpy as jnp
from jax import lax
from jax.experimental import pallas as pl
from jax.experimental.pallas import tpu as pltpu
from jax.sharding import PartitionSpec as P

D = 1152
HEADS = 16
HD = 72
BLK = 128
HALF = BLK // 2
DEVICES = 64
GROUPS = DEVICES // HEADS

IN_ROWS = 112
OUT_ROWS = 40
AUG = 80
TILES = 22
CHUNK = 2 * BLK
COLUMNS = (TILES - 1) * BLK
Q_TILES = (512, 640, 768, 672)
UNROLL = 17
EARLY = 64
MIB = 1024 * 1024

INVERSE = 1.0 / HD**0.5
LOG2E = 1.4426950408889634


def place_of(slots):
    return (slots & 1) * HALF + (slots >> 1)


def roll(x, shift):
    return pltpu.roll(x, shift, 1)


def pre_kernel(
    slots_ref,
    tokens_ref,
    shift_ref,
    scale_ref,
    w_ref,
    out_ref,
    slots_buf,
    tok_buf,
    shift_buf,
    scale_buf,
    w_buf,
    qkv_t,
    messages,
    in_sems,
    w_sems,
    out_sems,
):
    small = [
        pltpu.make_async_copy(src, dst, in_sems.at[i])
        for i, (src, dst) in enumerate(
            [
                (slots_ref, slots_buf),
                (tokens_ref, tok_buf),
                (shift_ref, shift_buf),
                (scale_ref, scale_buf),
            ]
        )
    ]
    for copy in small:
        copy.start()
    large = [
        pltpu.make_async_copy(w_ref.at[:, pl.ds(part * D, D)], w_buf.at[part], w_sems.at[part])
        for part in (1, 2, 0)
    ]
    for copy in large:
        copy.start()

    small[0].wait()
    place = jnp.broadcast_to(place_of(slots_buf[...]), (BLK, BLK))
    row_id = lax.broadcasted_iota(jnp.int32, (BLK, BLK), 0)
    hot = jnp.where(place == row_id, 1.0, 0.0)
    members = jnp.sum(hot, axis=1, keepdims=True)
    members_row = jnp.sum(hot.T, axis=0, keepdims=True)
    low = lax.broadcasted_iota(jnp.int32, (1, BLK), 1) < HALF
    line = lax.broadcasted_iota(jnp.int32, (8, BLK), 0)
    alive = jnp.where(members_row > 0.0, 1.0, 0.0)
    live = [
        jnp.sum(jnp.where(low == even, alive, 0.0), axis=1, keepdims=True) for even in (True, False)
    ]
    sizes_of = [roll(jnp.broadcast_to(members_row, (8, BLK)), HALF)]
    sizes_of.append(jnp.broadcast_to(members_row, (8, BLK)))
    sizes = [
        [
            jnp.where(
                line == 0,
                sizes_of[b],
                jnp.where(line == 1, live[b], jnp.where(line == 2, live[a], 0.0)),
            )
            for b in range(2)
        ]
        for a in range(2)
    ]

    for copy in small[1:]:
        copy.wait()
    sums = jnp.dot(hot.astype(jnp.bfloat16), tok_buf[...], preferred_element_type=jnp.float32)
    values = (sums / jnp.maximum(members, 1.0)).astype(jnp.bfloat16).astype(jnp.float32)
    center = jnp.mean(values, axis=-1, keepdims=True)
    off = values - center
    spread = jnp.mean(off * off, axis=-1, keepdims=True)
    normed = (off * lax.rsqrt(spread + 1e-06) * (1.0 + scale_buf[...]) + shift_buf[...]).astype(
        jnp.bfloat16
    )

    def project(part):
        out = jnp.dot(normed, w_buf[part], preferred_element_type=jnp.float32)
        for t in range(D // BLK):
            qkv_t[part, t * BLK : (t + 1) * BLK, :] = out[:, t * BLK : (t + 1) * BLK].T

    large[0].wait()
    large[1].wait()
    project(1)
    project(2)
    large[2].wait()
    project(0)
    early = []
    for h in range(HEADS):
        k = qkv_t[1, h * HD : (h + 1) * HD, :]
        v = qkv_t[2, h * HD : (h + 1) * HD, :]
        kv = [jnp.where(low, k, roll(v, HALF)), jnp.where(low, roll(k, HALF), v)]
        early.append([x[EARLY:] for x in kv])
        for a in range(2):
            for b in range(2):
                messages[h * GROUPS + 2 * a + b, :EARLY, :] = kv[b][:EARLY].astype(jnp.bfloat16)
    first = pltpu.make_async_copy(
        messages.at[:, pl.ds(0, EARLY)], out_ref.at[:, pl.ds(0, EARLY)], out_sems.at[0]
    )
    first.start()
    for h in range(HEADS):
        q = qkv_t[0, h * HD : (h + 1) * HD, :]
        q_roll = roll(q, HALF)
        q_pair = [
            jnp.where(low, q[:32], q_roll[32:64]),
            jnp.where(low, q_roll[:32], q[32:64]),
        ]
        q_last = [q[64:], q_roll[64:]]
        for a in range(2):
            for b in range(2):
                last = jnp.where(low, q_last[a], sizes[a][b])
                messages[h * GROUPS + 2 * a + b, EARLY:, :] = jnp.concatenate(
                    [early[h][b], q_pair[a], last], axis=0
                ).astype(jnp.bfloat16)
    second = pltpu.make_async_copy(
        messages.at[:, pl.ds(EARLY, IN_ROWS - EARLY)],
        out_ref.at[:, pl.ds(EARLY, IN_ROWS - EARLY)],
        out_sems.at[1],
    )
    second.start()
    first.wait()
    second.wait()


def attend_kernel(
    got,
    out,
    offs_v,
    offs,
    k_t,
    v_t,
    q_t,
    keys,
    vals,
    queries,
    scores_a,
    scores_b,
    top_a,
    top_b,
    done,
    done_t,
    sem,
):
    lane = lax.broadcasted_iota(jnp.int32, (1, BLK), 1)
    low = lane < HALF

    row = lax.broadcasted_iota(jnp.int32, (BLK, DEVICES * 16), 0)
    col = lax.broadcasted_iota(jnp.int32, (BLK, DEVICES * 16), 1)
    last_rows = got[:, IN_ROWS - 16 :, :].reshape(DEVICES * 16, BLK)
    for x in range(2):
        before = (col < row * 16) & ((col & 15) == 9 + x)
        sums = jnp.dot(
            jnp.where(before, 1.0, 0.0).astype(jnp.bfloat16),
            last_rows,
            preferred_element_type=jnp.float32,
        )
        offs_v[8 * x : 8 * x + 8, :] = sums.T[HALF : HALF + 8].astype(jnp.int32)
    copy = pltpu.make_async_copy(offs_v, offs, sem)
    copy.start()
    copy.wait()

    def put(dst, tile, first, last, moved, keep):
        dst[tile, first:last, :] = jnp.where(keep, moved, dst[tile, first:last, :])
        dst[tile + 1, first:last, :] = moved

    k_t[0] = jnp.zeros_like(k_t[0])
    v_t[0] = jnp.zeros_like(v_t[0])
    q_t[0] = jnp.zeros_like(q_t[0])

    def pack(b, _):
        k_at = offs[0, b]
        q_at = offs[8, b]
        k_tile, k_off = k_at >> 7, k_at & 127
        q_tile, q_off = q_at >> 7, q_at & 127
        message = got[b].astype(jnp.float32)
        keep_k, keep_q = lane >= k_off, lane >= q_off
        k_over, q_over = (k_off + HALF) & 127, (q_off + HALF) & 127
        put(k_t, k_tile, 0, HD, roll(message[:HD], k_off), keep_k)
        put(k_t, k_tile, HD, AUG, roll(message[104:], k_over), keep_k)
        put(q_t, q_tile, 0, 32, roll(message[HD:104], q_off), keep_q)
        put(q_t, q_tile, 32, 64, roll(message[HD:104], q_over), keep_q)
        put(q_t, q_tile, 64, HD, roll(message[104:], q_off), keep_q)
        return 0

    def pack_values(b):
        at = offs[0, b]
        tile, off = at >> 7, at & 127
        moved = roll(got[b, :HD, :].astype(jnp.float32), (off + HALF) & 127)
        put(v_t, tile, 0, HD, moved, lane >= off)

    lax.fori_loop(0, DEVICES, pack, 0, unroll=32)

    total = offs[0, DEVICES]
    line8 = lax.broadcasted_iota(jnp.int32, (8, BLK), 0)
    zeros = jnp.zeros((BLK - AUG, BLK), jnp.float32)
    ones2 = jnp.where(line8 < 2, 1.0, 0.0)
    ones1 = jnp.where(line8 < 1, 1.0, 0.0)
    def set_keys(t):
        members = jnp.broadcast_to(k_t[t, HD : HD + 1, :], (8, BLK))
        bias = jnp.log(jnp.maximum(members, 1.0)) * (1.0 / INVERSE)
        bias = jnp.where(lane + t * BLK < total, bias, -1e30)
        high = bias.astype(jnp.bfloat16).astype(jnp.float32)
        rest = jnp.where(line8 == 0, high, jnp.where(line8 == 1, bias - high, 0.0))
        keys[:, t * BLK : (t + 1) * BLK] = jnp.concatenate(
            [k_t[t, :HD, :], rest, zeros], axis=0
        ).astype(jnp.bfloat16)

    def set_queries(t):
        queries[t * BLK : (t + 1) * BLK, :] = jnp.concatenate(
            [q_t[t, :HD, :], ones2, zeros], axis=0
        ).T.astype(jnp.bfloat16)

    def set_values(t):
        vals[t * BLK : (t + 1) * BLK, :] = jnp.concatenate(
            [v_t[t, :HD, :], ones1, zeros], axis=0
        ).T.astype(jnp.bfloat16)

    for t in range(TILES - 1):
        set_keys(t)
    early = Q_TILES[0] // BLK
    for t in range(early):
        set_queries(t)

    chunks = [slice(at, min(at + CHUNK, COLUMNS)) for at in range(0, COLUMNS, CHUNK)]
    starts = [sum(Q_TILES[:i]) for i in range(len(Q_TILES) + 1)]

    def fold(s, best):
        for t in range(s.shape[1] // BLK):
            part = s[:, t * BLK : (t + 1) * BLK]
            best = part if best is None else jnp.maximum(best, part)
        return best

    def turn(t):
        last = min((t + 1) * BLK, starts[-1])
        tile = done[t * BLK : last, :]
        if last < (t + 1) * BLK:
            tile = jnp.concatenate(
                [tile, jnp.zeros(((t + 1) * BLK - last, BLK), jnp.float32)], axis=0
            )
        done_t[t] = tile.T[:AUG]

    def unpack(b, _):
        at = offs[8, b]
        tile, off = at >> 7, at & 127
        both = jnp.where(lane >= off, done_t[tile], done_t[tile + 1])
        first = roll(both[:OUT_ROWS], (BLK - off) & 127)
        second = roll(both[OUT_ROWS:], (BLK + HALF - off) & 127)
        out[b] = jnp.where(low, first, second).astype(jnp.bfloat16)
        return 0

    def step(i, beside):
        scores, top = (scores_a, top_a) if i % 2 == 0 else (scores_b, top_b)
        ahead_scores, ahead_top = (scores_b, top_b) if i % 2 == 0 else (scores_a, top_a)
        n = Q_TILES[i] if i >= 0 else 0
        m = Q_TILES[i + 1] if i + 1 < len(Q_TILES) else 0
        best = None
        o = None
        q = queries[starts[i + 1] : starts[i + 1] + m, :] if m else None
        each = -(-len(beside) // len(chunks))
        for x, c in enumerate(chunks):
            for work in beside[x * each : (x + 1) * each]:
                work()
            if m:
                s = jnp.dot(q, keys[:, c], preferred_element_type=jnp.float32)
                ahead_scores[:m, c] = s
                best = fold(s, best)
            if n:
                p = [
                    jnp.exp2(
                        (scores[:n, at : at + BLK] - top[:n]) * (INVERSE * LOG2E)
                    ).astype(jnp.bfloat16)
                    for at in range(c.start, c.stop, BLK)
                ]
                p = jnp.concatenate(p, axis=1)
                part = jnp.dot(p, vals[c, :], preferred_element_type=jnp.float32)
                o = part if o is None else o + part
        if m:
            ahead_top[:m] = jnp.broadcast_to(jnp.max(best, axis=1, keepdims=True), (m, BLK))
        if n:
            mass = jnp.broadcast_to(o[:, HD : HD + 1], (n, BLK))
            lse = top[:n] * INVERSE + jnp.log(mass)
            high = lse.astype(jnp.bfloat16).astype(jnp.float32)
            done[starts[i] : starts[i + 1], :] = jnp.where(
                lane < HD, o / mass, jnp.where(lane == HD, high, lse - high)
            )

    turned = 0
    unpacked = 0
    done_t[TILES - 1] = jnp.zeros((AUG, BLK), jnp.float32)
    for i in range(-1, len(Q_TILES)):
        beside = []
        if i < 0:
            beside += [functools.partial(pack_values, b) for b in range(DEVICES)]
            beside += [functools.partial(set_queries, t) for t in range(early, TILES - 1)]
            beside += [functools.partial(set_values, t) for t in range(TILES - 1)]
        if i >= 1:
            for t in range(turned, starts[i] // BLK):
                beside.append(functools.partial(turn, t))
            turned = starts[i] // BLK
            for b in range(unpacked, turned * BLK // HALF):
                beside.append(functools.partial(unpack, b, 0))
            unpacked = turned * BLK // HALF
        step(i, beside)
    for t in range(turned, TILES - 1):
        turn(t)
    lax.fori_loop(unpacked, DEVICES, unpack, 0, unroll=UNROLL)


def post_kernel(got, slots_ref, tokens_ref, gate_ref, w_ref, out_ref, att_t):
    place = jnp.broadcast_to(place_of(slots_ref[...]), (BLK, BLK))
    row_id = lax.broadcasted_iota(jnp.int32, (BLK, BLK), 0)
    hot = jnp.where(place == row_id, 1.0, 0.0).T.astype(jnp.bfloat16)
    low = lax.broadcasted_iota(jnp.int32, (1, BLK), 1) < HALF
    for h in range(HEADS):
        halves = []
        for a in range(2):
            parts = [got[h * GROUPS + 2 * a + b].astype(jnp.float32) for b in range(2)]
            lse = [p[32:33] + p[33:34] for p in parts]
            gap = jnp.broadcast_to(lse[1] - lse[0], (8, BLK))
            gap = jnp.where(low, roll(gap, HALF), gap)[:1]
            share = 1.0 / (1.0 + jnp.exp(gap))
            halves.append(parts[0] * share + parts[1] * (1.0 - share))
        x, y = halves
        upper = jnp.where(low, x, roll(y, HALF))
        lower = jnp.where(low, roll(x, HALF), y)
        att_t[h * HD : (h + 1) * HD, :] = jnp.concatenate(
            [upper, lower[: HD - OUT_ROWS]], axis=0
        )
    rows = lax.dot_general(
        hot,
        att_t[...].astype(jnp.bfloat16),
        (((1,), (1,)), ((), ())),
        preferred_element_type=jnp.float32,
    ).astype(jnp.bfloat16)
    branch = jnp.dot(rows, w_ref[...], preferred_element_type=jnp.float32)
    out_ref[...] = (tokens_ref[...].astype(jnp.float32) + gate_ref[...] * branch).astype(
        jnp.bfloat16
    )


def vmem():
    return pl.BlockSpec(memory_space=pltpu.VMEM)


def hbm():
    return pl.BlockSpec(memory_space=pl.ANY)


def pre(slots, tokens, shift, scale, w_qkv):
    return pl.pallas_call(
        pre_kernel,
        out_shape=jax.ShapeDtypeStruct((DEVICES, IN_ROWS, BLK), jnp.bfloat16),
        in_specs=[hbm()] * 5,
        out_specs=hbm(),
        scratch_shapes=[
            pltpu.VMEM((BLK,), jnp.int32),
            pltpu.VMEM((BLK, D), jnp.bfloat16),
            pltpu.VMEM((D,), jnp.float32),
            pltpu.VMEM((D,), jnp.float32),
            pltpu.VMEM((3, D, D), jnp.bfloat16),
            pltpu.VMEM((3, D, BLK), jnp.float32),
            pltpu.VMEM((DEVICES, IN_ROWS, BLK), jnp.bfloat16),
            pltpu.SemaphoreType.DMA((4,)),
            pltpu.SemaphoreType.DMA((3,)),
            pltpu.SemaphoreType.DMA((2,)),
        ],
        compiler_params=pltpu.CompilerParams(vmem_limit_bytes=56 * MIB),
        name="merge_norm_qkv",
    )(slots, tokens, shift, scale, w_qkv)


def attend(got):
    return pl.pallas_call(
        attend_kernel,
        out_shape=jax.ShapeDtypeStruct((DEVICES, OUT_ROWS, BLK), jnp.bfloat16),
        in_specs=[vmem()],
        out_specs=vmem(),
        scratch_shapes=[
            pltpu.VMEM((16, BLK), jnp.int32),
            pltpu.SMEM((16, BLK), jnp.int32),
            pltpu.VMEM((TILES, AUG, BLK), jnp.float32),
            pltpu.VMEM((TILES, HD, BLK), jnp.float32),
            pltpu.VMEM((TILES, HD, BLK), jnp.float32),
            pltpu.VMEM((BLK, COLUMNS), jnp.bfloat16),
            pltpu.VMEM((COLUMNS, BLK), jnp.bfloat16),
            pltpu.VMEM((COLUMNS, BLK), jnp.bfloat16),
            pltpu.VMEM((max(Q_TILES), COLUMNS), jnp.float32),
            pltpu.VMEM((max(Q_TILES), COLUMNS), jnp.float32),
            pltpu.VMEM((max(Q_TILES), BLK), jnp.float32),
            pltpu.VMEM((max(Q_TILES), BLK), jnp.float32),
            pltpu.VMEM((sum(Q_TILES), BLK), jnp.float32),
            pltpu.VMEM((TILES, AUG, BLK), jnp.float32),
            pltpu.SemaphoreType.DMA,
        ],
        compiler_params=pltpu.CompilerParams(vmem_limit_bytes=30 * MIB),
        name="attend_head",
    )(got)


def post(returned, slots, tokens, gate, w_out):
    return pl.pallas_call(
        post_kernel,
        out_shape=jax.ShapeDtypeStruct((BLK, D), jnp.bfloat16),
        in_specs=[vmem()] * 5,
        out_specs=vmem(),
        scratch_shapes=[pltpu.VMEM((D, BLK), jnp.float32)],
        compiler_params=pltpu.CompilerParams(vmem_limit_bytes=8 * MIB),
        name="combine_project",
    )(returned, slots, tokens, gate, w_out)


def body(tokens, slots, counts, shift, scale, gate, w_qkv, w_out):
    sent = pre(slots, tokens, shift, scale, w_qkv)
    got = lax.all_to_all(sent, "patch", 0, 0, tiled=True)
    back = attend(got)
    returned = lax.all_to_all(back, "patch", 0, 0, tiled=True)
    return post(returned, slots, tokens, gate, w_out)


def solution(mesh):
    split = ("batch", "patch")
    return jax.shard_map(
        body,
        mesh=mesh,
        in_specs=(P(split, None), P(split), P(split), P(), P(), P(), P(), P()),
        out_specs=P(split, None),
        check_vma=False,
    )
```

```python
import functools

import jax
import jax.numpy as jnp
from jax import lax
from jax.experimental import pallas as pl
from jax.experimental.pallas import tpu as pltpu
from jax.sharding import PartitionSpec as P

D = 1152
HEADS = 16
HD = 72
BLK = 128
HALF = BLK // 2
DEVICES = 64
GROUPS = DEVICES // HEADS

IN_ROWS = 112
OUT_ROWS = 40
AUG = 80
TILES = 22
CHUNK = 4 * BLK
COLUMNS = (TILES - 1) * BLK
Q_TILES = (512, 640, 768, 672)
UNROLL = 17
EARLY = 64
MIB = 1024 * 1024

INVERSE = 1.0 / HD**0.5
LOG2E = 1.4426950408889634


def place_of(slots):
    return (slots & 1) * HALF + (slots >> 1)


def roll(x, shift):
    return pltpu.roll(x, shift, 1)


def pre_kernel(
    slots_ref,
    tokens_ref,
    shift_ref,
    scale_ref,
    w_ref,
    out_ref,
    slots_buf,
    tok_buf,
    shift_buf,
    scale_buf,
    w_buf,
    qkv_t,
    messages,
    in_sems,
    w_sems,
    out_sems,
):
    small = [
        pltpu.make_async_copy(src, dst, in_sems.at[i])
        for i, (src, dst) in enumerate(
            [
                (slots_ref, slots_buf),
                (tokens_ref, tok_buf),
                (shift_ref, shift_buf),
                (scale_ref, scale_buf),
            ]
        )
    ]
    for copy in small:
        copy.start()
    large = [
        pltpu.make_async_copy(w_ref.at[:, pl.ds(part * D, D)], w_buf.at[part], w_sems.at[part])
        for part in (1, 2, 0)
    ]
    large[0].start()
    large[1].start()

    small[0].wait()
    place = jnp.broadcast_to(place_of(slots_buf[...]), (BLK, BLK))
    row_id = lax.broadcasted_iota(jnp.int32, (BLK, BLK), 0)
    hot = jnp.where(place == row_id, 1.0, 0.0)
    members = jnp.sum(hot, axis=1, keepdims=True)
    members_row = jnp.sum(hot.T, axis=0, keepdims=True)
    low = lax.broadcasted_iota(jnp.int32, (1, BLK), 1) < HALF
    line = lax.broadcasted_iota(jnp.int32, (8, BLK), 0)
    alive = jnp.where(members_row > 0.0, 1.0, 0.0)
    live = [
        jnp.sum(jnp.where(low == even, alive, 0.0), axis=1, keepdims=True) for even in (True, False)
    ]
    sizes_of = [roll(jnp.broadcast_to(members_row, (8, BLK)), HALF)]
    sizes_of.append(jnp.broadcast_to(members_row, (8, BLK)))
    sizes = [
        [
            jnp.where(
                line == 0,
                sizes_of[b],
                jnp.where(line == 1, live[b], jnp.where(line == 2, live[a], 0.0)),
            )
            for b in range(2)
        ]
        for a in range(2)
    ]

    for copy in small[1:]:
        copy.wait()
    large[2].start()
    sums = jnp.dot(hot.astype(jnp.bfloat16), tok_buf[...], preferred_element_type=jnp.float32)
    values = (sums / jnp.maximum(members, 1.0)).astype(jnp.bfloat16).astype(jnp.float32)
    center = jnp.mean(values, axis=-1, keepdims=True)
    off = values - center
    spread = jnp.mean(off * off, axis=-1, keepdims=True)
    normed = (off * lax.rsqrt(spread + 1e-06) * (1.0 + scale_buf[...]) + shift_buf[...]).astype(
        jnp.bfloat16
    )

    def project(part):
        out = jnp.dot(normed, w_buf[part], preferred_element_type=jnp.float32)
        for t in range(D // BLK):
            qkv_t[part, t * BLK : (t + 1) * BLK, :] = out[:, t * BLK : (t + 1) * BLK].T

    large[0].wait()
    large[1].wait()
    project(1)
    project(2)
    large[2].wait()
    project(0)
    early = []
    for h in range(HEADS):
        k = qkv_t[1, h * HD : (h + 1) * HD, :]
        v = qkv_t[2, h * HD : (h + 1) * HD, :]
        kv = [jnp.where(low, k, roll(v, HALF)), jnp.where(low, roll(k, HALF), v)]
        early.append([x[EARLY:] for x in kv])
        for a in range(2):
            for b in range(2):
                messages[h * GROUPS + 2 * a + b, :EARLY, :] = kv[b][:EARLY].astype(jnp.bfloat16)
    first = pltpu.make_async_copy(
        messages.at[:, pl.ds(0, EARLY)], out_ref.at[:, pl.ds(0, EARLY)], out_sems.at[0]
    )
    first.start()
    for h in range(HEADS):
        q = qkv_t[0, h * HD : (h + 1) * HD, :]
        q_roll = roll(q, HALF)
        q_pair = [
            jnp.where(low, q[:32], q_roll[32:64]),
            jnp.where(low, q_roll[:32], q[32:64]),
        ]
        q_last = [q[64:], q_roll[64:]]
        for a in range(2):
            for b in range(2):
                last = jnp.where(low, q_last[a], sizes[a][b])
                messages[h * GROUPS + 2 * a + b, EARLY:, :] = jnp.concatenate(
                    [early[h][b], q_pair[a], last], axis=0
                ).astype(jnp.bfloat16)
    second = pltpu.make_async_copy(
        messages.at[:, pl.ds(EARLY, IN_ROWS - EARLY)],
        out_ref.at[:, pl.ds(EARLY, IN_ROWS - EARLY)],
        out_sems.at[1],
    )
    second.start()
    first.wait()
    second.wait()


def attend_kernel(
    got,
    out,
    offs_v,
    offs,
    k_t,
    v_t,
    q_t,
    keys,
    vals,
    queries,
    scores_a,
    scores_b,
    top_a,
    top_b,
    done,
    done_t,
    sem,
):
    lane = lax.broadcasted_iota(jnp.int32, (1, BLK), 1)
    low = lane < HALF

    row = lax.broadcasted_iota(jnp.int32, (BLK, DEVICES * 16), 0)
    col = lax.broadcasted_iota(jnp.int32, (BLK, DEVICES * 16), 1)
    last_rows = got[:, IN_ROWS - 16 :, :].reshape(DEVICES * 16, BLK)
    for x in range(2):
        before = (col < row * 16) & ((col & 15) == 9 + x)
        sums = jnp.dot(
            jnp.where(before, 1.0, 0.0).astype(jnp.bfloat16),
            last_rows,
            preferred_element_type=jnp.float32,
        )
        offs_v[8 * x : 8 * x + 8, :] = sums.T[HALF : HALF + 8].astype(jnp.int32)
    copy = pltpu.make_async_copy(offs_v, offs, sem)
    copy.start()
    copy.wait()

    def put(dst, tile, first, last, moved, keep):
        dst[tile, first:last, :] = jnp.where(keep, moved, dst[tile, first:last, :])
        dst[tile + 1, first:last, :] = moved

    k_t[0] = jnp.zeros_like(k_t[0])
    v_t[0] = jnp.zeros_like(v_t[0])
    q_t[0] = jnp.zeros_like(q_t[0])

    def pack(b, _):
        k_at = offs[0, b]
        q_at = offs[8, b]
        k_tile, k_off = k_at >> 7, k_at & 127
        q_tile, q_off = q_at >> 7, q_at & 127
        message = got[b].astype(jnp.float32)
        keep_k, keep_q = lane >= k_off, lane >= q_off
        k_over, q_over = (k_off + HALF) & 127, (q_off + HALF) & 127
        put(k_t, k_tile, 0, HD, roll(message[:HD], k_off), keep_k)
        put(k_t, k_tile, HD, AUG, roll(message[104:], k_over), keep_k)
        put(q_t, q_tile, 0, 32, roll(message[HD:104], q_off), keep_q)
        put(q_t, q_tile, 32, 64, roll(message[HD:104], q_over), keep_q)
        put(q_t, q_tile, 64, HD, roll(message[104:], q_off), keep_q)
        return 0

    def pack_values(b):
        at = offs[0, b]
        tile, off = at >> 7, at & 127
        moved = roll(got[b, :HD, :].astype(jnp.float32), (off + HALF) & 127)
        put(v_t, tile, 0, HD, moved, lane >= off)

    lax.fori_loop(0, DEVICES, pack, 0, unroll=32)

    total = offs[0, DEVICES]
    line8 = lax.broadcasted_iota(jnp.int32, (8, BLK), 0)
    zeros = jnp.zeros((BLK - AUG, BLK), jnp.float32)
    ones2 = jnp.where(line8 < 2, 1.0, 0.0)
    ones1 = jnp.where(line8 < 1, 1.0, 0.0)
    def set_keys(t):
        members = jnp.broadcast_to(k_t[t, HD : HD + 1, :], (8, BLK))
        bias = jnp.log(jnp.maximum(members, 1.0)) * (1.0 / INVERSE)
        bias = jnp.where(lane + t * BLK < total, bias, -1e30)
        high = bias.astype(jnp.bfloat16).astype(jnp.float32)
        rest = jnp.where(line8 == 0, high, jnp.where(line8 == 1, bias - high, 0.0))
        keys[:, t * BLK : (t + 1) * BLK] = jnp.concatenate(
            [k_t[t, :HD, :], rest, zeros], axis=0
        ).astype(jnp.bfloat16)

    def set_queries(t):
        queries[t * BLK : (t + 1) * BLK, :] = jnp.concatenate(
            [q_t[t, :HD, :], ones2, zeros], axis=0
        ).T.astype(jnp.bfloat16)

    def set_values(t):
        vals[t * BLK : (t + 1) * BLK, :] = jnp.concatenate(
            [v_t[t, :HD, :], ones1, zeros], axis=0
        ).T.astype(jnp.bfloat16)

    for t in range(TILES - 1):
        set_keys(t)
    early = Q_TILES[0] // BLK
    for t in range(early):
        set_queries(t)

    chunks = [slice(at, min(at + CHUNK, COLUMNS)) for at in range(0, COLUMNS, CHUNK)]
    starts = [sum(Q_TILES[:i]) for i in range(len(Q_TILES) + 1)]

    def fold(s, best):
        for t in range(s.shape[1] // BLK):
            part = s[:, t * BLK : (t + 1) * BLK]
            best = part if best is None else jnp.maximum(best, part)
        return best

    def turn(t):
        last = min((t + 1) * BLK, starts[-1])
        tile = done[t * BLK : last, :]
        if last < (t + 1) * BLK:
            tile = jnp.concatenate(
                [tile, jnp.zeros(((t + 1) * BLK - last, BLK), jnp.float32)], axis=0
            )
        done_t[t] = tile.T[:AUG]

    def unpack(b, _):
        at = offs[8, b]
        tile, off = at >> 7, at & 127
        both = jnp.where(lane >= off, done_t[tile], done_t[tile + 1])
        first = roll(both[:OUT_ROWS], (BLK - off) & 127)
        second = roll(both[OUT_ROWS:], (BLK + HALF - off) & 127)
        out[b] = jnp.where(low, first, second).astype(jnp.bfloat16)
        return 0

    def step(i, beside):
        scores, top = (scores_a, top_a) if i % 2 == 0 else (scores_b, top_b)
        ahead_scores, ahead_top = (scores_b, top_b) if i % 2 == 0 else (scores_a, top_a)
        n = Q_TILES[i] if i >= 0 else 0
        m = Q_TILES[i + 1] if i + 1 < len(Q_TILES) else 0
        best = None
        o = None
        q = queries[starts[i + 1] : starts[i + 1] + m, :] if m else None
        each = -(-len(beside) // len(chunks))
        for x, c in enumerate(chunks):
            for work in beside[x * each : (x + 1) * each]:
                work()
            if m:
                s = jnp.dot(q, keys[:, c], preferred_element_type=jnp.float32)
                ahead_scores[:m, c] = s
                best = fold(s, best)
            if n:
                p = [
                    jnp.exp2(
                        (scores[:n, at : at + BLK] - top[:n]) * (INVERSE * LOG2E)
                    ).astype(jnp.bfloat16)
                    for at in range(c.start, c.stop, BLK)
                ]
                p = jnp.concatenate(p, axis=1)
                part = jnp.dot(p, vals[c, :], preferred_element_type=jnp.float32)
                o = part if o is None else o + part
        if m:
            ahead_top[:m] = jnp.broadcast_to(jnp.max(best, axis=1, keepdims=True), (m, BLK))
        if n:
            mass = jnp.broadcast_to(o[:, HD : HD + 1], (n, BLK))
            lse = top[:n] * INVERSE + jnp.log(mass)
            high = lse.astype(jnp.bfloat16).astype(jnp.float32)
            done[starts[i] : starts[i + 1], :] = jnp.where(
                lane < HD, o / mass, jnp.where(lane == HD, high, lse - high)
            )

    turned = 0
    unpacked = 0
    done_t[TILES - 1] = jnp.zeros((AUG, BLK), jnp.float32)
    for i in range(-1, len(Q_TILES)):
        beside = []
        if i < 0:
            beside += [functools.partial(pack_values, b) for b in range(DEVICES)]
            beside += [functools.partial(set_queries, t) for t in range(early, TILES - 1)]
            beside += [functools.partial(set_values, t) for t in range(TILES - 1)]
        if i >= 1:
            for t in range(turned, starts[i] // BLK):
                beside.append(functools.partial(turn, t))
            turned = starts[i] // BLK
            for b in range(unpacked, turned * BLK // HALF):
                beside.append(functools.partial(unpack, b, 0))
            unpacked = turned * BLK // HALF
        step(i, beside)
    for t in range(turned, TILES - 1):
        turn(t)
    lax.fori_loop(unpacked, DEVICES, unpack, 0, unroll=UNROLL)


def post_kernel(got, slots_ref, tokens_ref, gate_ref, w_ref, out_ref, att_t):
    place = jnp.broadcast_to(place_of(slots_ref[...]), (BLK, BLK))
    row_id = lax.broadcasted_iota(jnp.int32, (BLK, BLK), 0)
    hot = jnp.where(place == row_id, 1.0, 0.0).T.astype(jnp.bfloat16)
    low = lax.broadcasted_iota(jnp.int32, (1, BLK), 1) < HALF
    for h in range(HEADS):
        halves = []
        for a in range(2):
            parts = [got[h * GROUPS + 2 * a + b].astype(jnp.float32) for b in range(2)]
            lse = [p[32:33] + p[33:34] for p in parts]
            gap = jnp.broadcast_to(lse[1] - lse[0], (8, BLK))
            gap = jnp.where(low, roll(gap, HALF), gap)[:1]
            share = 1.0 / (1.0 + jnp.exp(gap))
            halves.append(parts[0] * share + parts[1] * (1.0 - share))
        x, y = halves
        upper = jnp.where(low, x, roll(y, HALF))
        lower = jnp.where(low, roll(x, HALF), y)
        att_t[h * HD : (h + 1) * HD, :] = jnp.concatenate(
            [upper, lower[: HD - OUT_ROWS]], axis=0
        )
    rows = lax.dot_general(
        hot,
        att_t[...].astype(jnp.bfloat16),
        (((1,), (1,)), ((), ())),
        preferred_element_type=jnp.float32,
    ).astype(jnp.bfloat16)
    branch = jnp.dot(rows, w_ref[...], preferred_element_type=jnp.float32)
    out_ref[...] = (tokens_ref[...].astype(jnp.float32) + gate_ref[...] * branch).astype(
        jnp.bfloat16
    )


def vmem():
    return pl.BlockSpec(memory_space=pltpu.VMEM)


def hbm():
    return pl.BlockSpec(memory_space=pl.ANY)


def pre(slots, tokens, shift, scale, w_qkv):
    return pl.pallas_call(
        pre_kernel,
        out_shape=jax.ShapeDtypeStruct((DEVICES, IN_ROWS, BLK), jnp.bfloat16),
        in_specs=[hbm()] * 5,
        out_specs=hbm(),
        scratch_shapes=[
            pltpu.VMEM((BLK,), jnp.int32),
            pltpu.VMEM((BLK, D), jnp.bfloat16),
            pltpu.VMEM((D,), jnp.float32),
            pltpu.VMEM((D,), jnp.float32),
            pltpu.VMEM((3, D, D), jnp.bfloat16),
            pltpu.VMEM((3, D, BLK), jnp.float32),
            pltpu.VMEM((DEVICES, IN_ROWS, BLK), jnp.bfloat16),
            pltpu.SemaphoreType.DMA((4,)),
            pltpu.SemaphoreType.DMA((3,)),
            pltpu.SemaphoreType.DMA((2,)),
        ],
        compiler_params=pltpu.CompilerParams(vmem_limit_bytes=56 * MIB),
        name="merge_norm_qkv",
    )(slots, tokens, shift, scale, w_qkv)


def attend(got):
    return pl.pallas_call(
        attend_kernel,
        out_shape=jax.ShapeDtypeStruct((DEVICES, OUT_ROWS, BLK), jnp.bfloat16),
        in_specs=[vmem()],
        out_specs=vmem(),
        scratch_shapes=[
            pltpu.VMEM((16, BLK), jnp.int32),
            pltpu.SMEM((16, BLK), jnp.int32),
            pltpu.VMEM((TILES, AUG, BLK), jnp.float32),
            pltpu.VMEM((TILES, HD, BLK), jnp.float32),
            pltpu.VMEM((TILES, HD, BLK), jnp.float32),
            pltpu.VMEM((BLK, COLUMNS), jnp.bfloat16),
            pltpu.VMEM((COLUMNS, BLK), jnp.bfloat16),
            pltpu.VMEM((COLUMNS, BLK), jnp.bfloat16),
            pltpu.VMEM((max(Q_TILES), COLUMNS), jnp.float32),
            pltpu.VMEM((max(Q_TILES), COLUMNS), jnp.float32),
            pltpu.VMEM((max(Q_TILES), BLK), jnp.float32),
            pltpu.VMEM((max(Q_TILES), BLK), jnp.float32),
            pltpu.VMEM((sum(Q_TILES), BLK), jnp.float32),
            pltpu.VMEM((TILES, AUG, BLK), jnp.float32),
            pltpu.SemaphoreType.DMA,
        ],
        compiler_params=pltpu.CompilerParams(vmem_limit_bytes=30 * MIB),
        name="attend_head",
    )(got)


def post(returned, slots, tokens, gate, w_out):
    return pl.pallas_call(
        post_kernel,
        out_shape=jax.ShapeDtypeStruct((BLK, D), jnp.bfloat16),
        in_specs=[vmem()] * 5,
        out_specs=vmem(),
        scratch_shapes=[pltpu.VMEM((D, BLK), jnp.float32)],
        compiler_params=pltpu.CompilerParams(vmem_limit_bytes=8 * MIB),
        name="combine_project",
    )(returned, slots, tokens, gate, w_out)


def body(tokens, slots, counts, shift, scale, gate, w_qkv, w_out):
    sent = pre(slots, tokens, shift, scale, w_qkv)
    got = lax.all_to_all(sent, "patch", 0, 0, tiled=True)
    back = attend(got)
    returned = lax.all_to_all(back, "patch", 0, 0, tiled=True)
    return post(returned, slots, tokens, gate, w_out)


def solution(mesh):
    split = ("batch", "patch")
    return jax.shard_map(
        body,
        mesh=mesh,
        in_specs=(P(split, None), P(split), P(split), P(), P(), P(), P(), P()),
        out_specs=P(split, None),
        check_vma=False,
    )
```

```python
import functools

import jax
import jax.numpy as jnp
from jax import lax
from jax.experimental import pallas as pl
from jax.experimental.pallas import tpu as pltpu
from jax.sharding import PartitionSpec as P

D = 1152
HEADS = 16
HD = 72
BLK = 128
HALF = BLK // 2
DEVICES = 64
GROUPS = DEVICES // HEADS

IN_ROWS = 112
OUT_ROWS = 40
AUG = 80
TILES = 22
CHUNK = 4 * BLK
COLUMNS = (TILES - 1) * BLK
Q_TILES = (512, 896, 768, 416)
UNROLL = 30
EARLY = 64
MIB = 1024 * 1024

INVERSE = 1.0 / HD**0.5
LOG2E = 1.4426950408889634


def place_of(slots):
    return (slots & 1) * HALF + (slots >> 1)


def roll(x, shift):
    return pltpu.roll(x, shift, 1)


def pre_kernel(
    slots_ref,
    tokens_ref,
    shift_ref,
    scale_ref,
    w_ref,
    out_ref,
    slots_buf,
    tok_buf,
    shift_buf,
    scale_buf,
    w_buf,
    qkv_t,
    messages,
    in_sems,
    w_sems,
    out_sems,
):
    small = [
        pltpu.make_async_copy(src, dst, in_sems.at[i])
        for i, (src, dst) in enumerate(
            [
                (slots_ref, slots_buf),
                (tokens_ref, tok_buf),
                (shift_ref, shift_buf),
                (scale_ref, scale_buf),
            ]
        )
    ]
    for copy in small:
        copy.start()
    large = [
        pltpu.make_async_copy(w_ref.at[:, pl.ds(part * D, D)], w_buf.at[part], w_sems.at[part])
        for part in (1, 2, 0)
    ]
    large[0].start()
    large[1].start()

    small[0].wait()
    place = jnp.broadcast_to(place_of(slots_buf[...]), (BLK, BLK))
    row_id = lax.broadcasted_iota(jnp.int32, (BLK, BLK), 0)
    hot = jnp.where(place == row_id, 1.0, 0.0)
    members = jnp.sum(hot, axis=1, keepdims=True)
    members_row = jnp.sum(hot.T, axis=0, keepdims=True)
    low = lax.broadcasted_iota(jnp.int32, (1, BLK), 1) < HALF
    line = lax.broadcasted_iota(jnp.int32, (8, BLK), 0)
    alive = jnp.where(members_row > 0.0, 1.0, 0.0)
    live = [
        jnp.sum(jnp.where(low == even, alive, 0.0), axis=1, keepdims=True) for even in (True, False)
    ]
    sizes_of = [roll(jnp.broadcast_to(members_row, (8, BLK)), HALF)]
    sizes_of.append(jnp.broadcast_to(members_row, (8, BLK)))
    sizes = [
        [
            jnp.where(
                line == 0,
                sizes_of[b],
                jnp.where(line == 1, live[b], jnp.where(line == 2, live[a], 0.0)),
            )
            for b in range(2)
        ]
        for a in range(2)
    ]

    for copy in small[1:]:
        copy.wait()
    large[2].start()
    sums = jnp.dot(hot.astype(jnp.bfloat16), tok_buf[...], preferred_element_type=jnp.float32)
    values = (sums / jnp.maximum(members, 1.0)).astype(jnp.bfloat16).astype(jnp.float32)
    center = jnp.mean(values, axis=-1, keepdims=True)
    off = values - center
    spread = jnp.mean(off * off, axis=-1, keepdims=True)
    normed = (off * lax.rsqrt(spread + 1e-06) * (1.0 + scale_buf[...]) + shift_buf[...]).astype(
        jnp.bfloat16
    )

    def project(part):
        out = jnp.dot(normed, w_buf[part], preferred_element_type=jnp.float32)
        for t in range(D // BLK):
            qkv_t[part, t * BLK : (t + 1) * BLK, :] = out[:, t * BLK : (t + 1) * BLK].T

    large[0].wait()
    large[1].wait()
    project(1)
    project(2)
    large[2].wait()
    project(0)
    early = []
    for h in range(HEADS):
        k = qkv_t[1, h * HD : (h + 1) * HD, :]
        v = qkv_t[2, h * HD : (h + 1) * HD, :]
        kv = [jnp.where(low, k, roll(v, HALF)), jnp.where(low, roll(k, HALF), v)]
        early.append([x[EARLY:] for x in kv])
        for a in range(2):
            for b in range(2):
                messages[h * GROUPS + 2 * a + b, :EARLY, :] = kv[b][:EARLY].astype(jnp.bfloat16)
    first = pltpu.make_async_copy(
        messages.at[:, pl.ds(0, EARLY)], out_ref.at[:, pl.ds(0, EARLY)], out_sems.at[0]
    )
    first.start()
    for h in range(HEADS):
        q = qkv_t[0, h * HD : (h + 1) * HD, :]
        q_roll = roll(q, HALF)
        q_pair = [
            jnp.where(low, q[:32], q_roll[32:64]),
            jnp.where(low, q_roll[:32], q[32:64]),
        ]
        q_last = [q[64:], q_roll[64:]]
        for a in range(2):
            for b in range(2):
                last = jnp.where(low, q_last[a], sizes[a][b])
                messages[h * GROUPS + 2 * a + b, EARLY:, :] = jnp.concatenate(
                    [early[h][b], q_pair[a], last], axis=0
                ).astype(jnp.bfloat16)
    second = pltpu.make_async_copy(
        messages.at[:, pl.ds(EARLY, IN_ROWS - EARLY)],
        out_ref.at[:, pl.ds(EARLY, IN_ROWS - EARLY)],
        out_sems.at[1],
    )
    second.start()
    first.wait()
    second.wait()


def attend_kernel(
    got,
    out,
    offs_v,
    offs,
    k_t,
    v_t,
    q_t,
    keys,
    vals,
    queries,
    scores_a,
    scores_b,
    top_a,
    top_b,
    done,
    done_t,
    sem,
):
    lane = lax.broadcasted_iota(jnp.int32, (1, BLK), 1)
    low = lane < HALF

    row = lax.broadcasted_iota(jnp.int32, (BLK, DEVICES * 16), 0)
    col = lax.broadcasted_iota(jnp.int32, (BLK, DEVICES * 16), 1)
    last_rows = got[:, IN_ROWS - 16 :, :].reshape(DEVICES * 16, BLK)
    for x in range(2):
        before = (col < row * 16) & ((col & 15) == 9 + x)
        sums = jnp.dot(
            jnp.where(before, 1.0, 0.0).astype(jnp.bfloat16),
            last_rows,
            preferred_element_type=jnp.float32,
        )
        offs_v[8 * x : 8 * x + 8, :] = sums.T[HALF : HALF + 8].astype(jnp.int32)
    copy = pltpu.make_async_copy(offs_v, offs, sem)
    copy.start()
    copy.wait()

    def put(dst, tile, first, last, moved, keep):
        dst[tile, first:last, :] = jnp.where(keep, moved, dst[tile, first:last, :])
        dst[tile + 1, first:last, :] = moved

    k_t[0] = jnp.zeros_like(k_t[0])
    v_t[0] = jnp.zeros_like(v_t[0])
    q_t[0] = jnp.zeros_like(q_t[0])

    def pack(b, _):
        k_at = offs[0, b]
        q_at = offs[8, b]
        k_tile, k_off = k_at >> 7, k_at & 127
        q_tile, q_off = q_at >> 7, q_at & 127
        message = got[b].astype(jnp.float32)
        keep_k, keep_q = lane >= k_off, lane >= q_off
        k_over, q_over = (k_off + HALF) & 127, (q_off + HALF) & 127
        put(k_t, k_tile, 0, HD, roll(message[:HD], k_off), keep_k)
        put(k_t, k_tile, HD, AUG, roll(message[104:], k_over), keep_k)
        put(q_t, q_tile, 0, 32, roll(message[HD:104], q_off), keep_q)
        put(q_t, q_tile, 32, 64, roll(message[HD:104], q_over), keep_q)
        put(q_t, q_tile, 64, HD, roll(message[104:], q_off), keep_q)
        return 0

    def pack_values(b):
        at = offs[0, b]
        tile, off = at >> 7, at & 127
        moved = roll(got[b, :HD, :].astype(jnp.float32), (off + HALF) & 127)
        put(v_t, tile, 0, HD, moved, lane >= off)

    lax.fori_loop(0, DEVICES, pack, 0, unroll=32)

    total = offs[0, DEVICES]
    line8 = lax.broadcasted_iota(jnp.int32, (8, BLK), 0)
    zeros = jnp.zeros((BLK - AUG, BLK), jnp.float32)
    ones2 = jnp.where(line8 < 2, 1.0, 0.0)
    ones1 = jnp.where(line8 < 1, 1.0, 0.0)
    def set_keys(t):
        members = jnp.broadcast_to(k_t[t, HD : HD + 1, :], (8, BLK))
        bias = jnp.log(jnp.maximum(members, 1.0)) * (1.0 / INVERSE)
        bias = jnp.where(lane + t * BLK < total, bias, -1e30)
        high = bias.astype(jnp.bfloat16).astype(jnp.float32)
        rest = jnp.where(line8 == 0, high, jnp.where(line8 == 1, bias - high, 0.0))
        keys[:, t * BLK : (t + 1) * BLK] = jnp.concatenate(
            [k_t[t, :HD, :], rest, zeros], axis=0
        ).astype(jnp.bfloat16)

    def set_queries(t):
        queries[t * BLK : (t + 1) * BLK, :] = jnp.concatenate(
            [q_t[t, :HD, :], ones2, zeros], axis=0
        ).T.astype(jnp.bfloat16)

    def set_values(t):
        vals[t * BLK : (t + 1) * BLK, :] = jnp.concatenate(
            [v_t[t, :HD, :], ones1, zeros], axis=0
        ).T.astype(jnp.bfloat16)

    for t in range(TILES - 1):
        set_keys(t)
    early = Q_TILES[0] // BLK
    for t in range(early):
        set_queries(t)

    chunks = [slice(at, min(at + CHUNK, COLUMNS)) for at in range(0, COLUMNS, CHUNK)]
    starts = [sum(Q_TILES[:i]) for i in range(len(Q_TILES) + 1)]

    def fold(s, best):
        for t in range(s.shape[1] // BLK):
            part = s[:, t * BLK : (t + 1) * BLK]
            best = part if best is None else jnp.maximum(best, part)
        return best

    def turn(t):
        last = min((t + 1) * BLK, starts[-1])
        tile = done[t * BLK : last, :]
        if last < (t + 1) * BLK:
            tile = jnp.concatenate(
                [tile, jnp.zeros(((t + 1) * BLK - last, BLK), jnp.float32)], axis=0
            )
        done_t[t] = tile.T[:AUG]

    def unpack(b, _):
        at = offs[8, b]
        tile, off = at >> 7, at & 127
        both = jnp.where(lane >= off, done_t[tile], done_t[tile + 1])
        first = roll(both[:OUT_ROWS], (BLK - off) & 127)
        second = roll(both[OUT_ROWS:], (BLK + HALF - off) & 127)
        out[b] = jnp.where(low, first, second).astype(jnp.bfloat16)
        return 0

    def step(i, beside):
        scores, top = (scores_a, top_a) if i % 2 == 0 else (scores_b, top_b)
        ahead_scores, ahead_top = (scores_b, top_b) if i % 2 == 0 else (scores_a, top_a)
        n = Q_TILES[i] if i >= 0 else 0
        m = Q_TILES[i + 1] if i + 1 < len(Q_TILES) else 0
        best = None
        o = None
        q = queries[starts[i + 1] : starts[i + 1] + m, :] if m else None
        each = -(-len(beside) // len(chunks))
        for x, c in enumerate(chunks):
            for work in beside[x * each : (x + 1) * each]:
                work()
            if m:
                s = jnp.dot(q, keys[:, c], preferred_element_type=jnp.float32)
                ahead_scores[:m, c] = s
                best = fold(s, best)
            if n:
                p = [
                    jnp.exp2(
                        (scores[:n, at : at + BLK] - top[:n]) * (INVERSE * LOG2E)
                    ).astype(jnp.bfloat16)
                    for at in range(c.start, c.stop, BLK)
                ]
                p = jnp.concatenate(p, axis=1)
                part = jnp.dot(p, vals[c, :], preferred_element_type=jnp.float32)
                o = part if o is None else o + part
        if m:
            ahead_top[:m] = jnp.broadcast_to(jnp.max(best, axis=1, keepdims=True), (m, BLK))
        if n:
            mass = jnp.broadcast_to(o[:, HD : HD + 1], (n, BLK))
            lse = top[:n] * INVERSE + jnp.log(mass)
            high = lse.astype(jnp.bfloat16).astype(jnp.float32)
            done[starts[i] : starts[i + 1], :] = jnp.where(
                lane < HD, o / mass, jnp.where(lane == HD, high, lse - high)
            )

    turned = 0
    unpacked = 0
    done_t[TILES - 1] = jnp.zeros((AUG, BLK), jnp.float32)
    for i in range(-1, len(Q_TILES)):
        beside = []
        if i < 0:
            beside += [functools.partial(pack_values, b) for b in range(DEVICES)]
            beside += [functools.partial(set_queries, t) for t in range(early, TILES - 1)]
            beside += [functools.partial(set_values, t) for t in range(TILES - 1)]
        if i >= 1:
            for t in range(turned, starts[i] // BLK):
                beside.append(functools.partial(turn, t))
            turned = starts[i] // BLK
            for b in range(unpacked, turned * BLK // HALF):
                beside.append(functools.partial(unpack, b, 0))
            unpacked = turned * BLK // HALF
        step(i, beside)
    for t in range(turned, TILES - 1):
        turn(t)
    lax.fori_loop(unpacked, DEVICES, unpack, 0, unroll=UNROLL)


def post_kernel(got, slots_ref, tokens_ref, gate_ref, w_ref, out_ref, att_t):
    place = jnp.broadcast_to(place_of(slots_ref[...]), (BLK, BLK))
    row_id = lax.broadcasted_iota(jnp.int32, (BLK, BLK), 0)
    hot = jnp.where(place == row_id, 1.0, 0.0).T.astype(jnp.bfloat16)
    low = lax.broadcasted_iota(jnp.int32, (1, BLK), 1) < HALF
    for h in range(HEADS):
        halves = []
        for a in range(2):
            parts = [got[h * GROUPS + 2 * a + b].astype(jnp.float32) for b in range(2)]
            lse = [p[32:33] + p[33:34] for p in parts]
            gap = jnp.broadcast_to(lse[1] - lse[0], (8, BLK))
            gap = jnp.where(low, roll(gap, HALF), gap)[:1]
            share = 1.0 / (1.0 + jnp.exp(gap))
            halves.append(parts[0] * share + parts[1] * (1.0 - share))
        x, y = halves
        upper = jnp.where(low, x, roll(y, HALF))
        lower = jnp.where(low, roll(x, HALF), y)
        att_t[h * HD : (h + 1) * HD, :] = jnp.concatenate(
            [upper, lower[: HD - OUT_ROWS]], axis=0
        )
    rows = lax.dot_general(
        hot,
        att_t[...].astype(jnp.bfloat16),
        (((1,), (1,)), ((), ())),
        preferred_element_type=jnp.float32,
    ).astype(jnp.bfloat16)
    branch = jnp.dot(rows, w_ref[...], preferred_element_type=jnp.float32)
    out_ref[...] = (tokens_ref[...].astype(jnp.float32) + gate_ref[...] * branch).astype(
        jnp.bfloat16
    )


def vmem():
    return pl.BlockSpec(memory_space=pltpu.VMEM)


def hbm():
    return pl.BlockSpec(memory_space=pl.ANY)


def pre(slots, tokens, shift, scale, w_qkv):
    return pl.pallas_call(
        pre_kernel,
        out_shape=jax.ShapeDtypeStruct((DEVICES, IN_ROWS, BLK), jnp.bfloat16),
        in_specs=[hbm()] * 5,
        out_specs=hbm(),
        scratch_shapes=[
            pltpu.VMEM((BLK,), jnp.int32),
            pltpu.VMEM((BLK, D), jnp.bfloat16),
            pltpu.VMEM((D,), jnp.float32),
            pltpu.VMEM((D,), jnp.float32),
            pltpu.VMEM((3, D, D), jnp.bfloat16),
            pltpu.VMEM((3, D, BLK), jnp.float32),
            pltpu.VMEM((DEVICES, IN_ROWS, BLK), jnp.bfloat16),
            pltpu.SemaphoreType.DMA((4,)),
            pltpu.SemaphoreType.DMA((3,)),
            pltpu.SemaphoreType.DMA((2,)),
        ],
        compiler_params=pltpu.CompilerParams(vmem_limit_bytes=56 * MIB),
        name="merge_norm_qkv",
    )(slots, tokens, shift, scale, w_qkv)


def attend(got):
    return pl.pallas_call(
        attend_kernel,
        out_shape=jax.ShapeDtypeStruct((DEVICES, OUT_ROWS, BLK), jnp.bfloat16),
        in_specs=[vmem()],
        out_specs=vmem(),
        scratch_shapes=[
            pltpu.VMEM((16, BLK), jnp.int32),
            pltpu.SMEM((16, BLK), jnp.int32),
            pltpu.VMEM((TILES, AUG, BLK), jnp.float32),
            pltpu.VMEM((TILES, HD, BLK), jnp.float32),
            pltpu.VMEM((TILES, HD, BLK), jnp.float32),
            pltpu.VMEM((BLK, COLUMNS), jnp.bfloat16),
            pltpu.VMEM((COLUMNS, BLK), jnp.bfloat16),
            pltpu.VMEM((COLUMNS, BLK), jnp.bfloat16),
            pltpu.VMEM((max(Q_TILES), COLUMNS), jnp.float32),
            pltpu.VMEM((max(Q_TILES), COLUMNS), jnp.float32),
            pltpu.VMEM((max(Q_TILES), BLK), jnp.float32),
            pltpu.VMEM((max(Q_TILES), BLK), jnp.float32),
            pltpu.VMEM((sum(Q_TILES), BLK), jnp.float32),
            pltpu.VMEM((TILES, AUG, BLK), jnp.float32),
            pltpu.SemaphoreType.DMA,
        ],
        compiler_params=pltpu.CompilerParams(vmem_limit_bytes=34 * MIB),
        name="attend_head",
    )(got)


def post(returned, slots, tokens, gate, w_out):
    return pl.pallas_call(
        post_kernel,
        out_shape=jax.ShapeDtypeStruct((BLK, D), jnp.bfloat16),
        in_specs=[vmem()] * 5,
        out_specs=vmem(),
        scratch_shapes=[pltpu.VMEM((D, BLK), jnp.float32)],
        compiler_params=pltpu.CompilerParams(vmem_limit_bytes=8 * MIB),
        name="combine_project",
    )(returned, slots, tokens, gate, w_out)


def body(tokens, slots, counts, shift, scale, gate, w_qkv, w_out):
    sent = pre(slots, tokens, shift, scale, w_qkv)
    got = lax.all_to_all(sent, "patch", 0, 0, tiled=True)
    back = attend(got)
    returned = lax.all_to_all(back, "patch", 0, 0, tiled=True)
    return post(returned, slots, tokens, gate, w_out)


def solution(mesh):
    split = ("batch", "patch")
    return jax.shard_map(
        body,
        mesh=mesh,
        in_specs=(P(split, None), P(split), P(split), P(), P(), P(), P(), P()),
        out_specs=P(split, None),
        check_vma=False,
    )
```
